256 devices in a mesh: dom: 256 (over z, y, x, core).
Axes of the slice: x: 4, y: 4, z: 8, core: 2. Of those that a mesh axis runs over, the one named last changes fastest.
Arguments:
- nodes: bfloat16 [262144, 128], P('dom'), may hold values from -6 to 6
- fine_edges: bfloat16 [2097152, 128], P('dom'), may hold values from -6 to 6
- fine_recv: int32 [16384, 128], P('dom'), may hold values from 0 to 127
- fine_send: int32 [16384, 128], P('dom'), may hold values from 0 to 1535
- fine_live: int32 [16384, 128], P('dom'), may hold values 0 or 1
- bound_rows: int32 [256, 512], P('dom'), may hold values from 0 to 1023
- cluster: int32 [262144], P('dom'), may hold values from 0 to 1023
- coarse_edges: bfloat16 [524288, 128], P('dom'), may hold values from -6 to 6
- coarse_recv: int32 [4096, 128], P('dom'), may hold values from 0 to 127
- coarse_send: int32 [4096, 128], P('dom'), may hold values from 0 to 1151, as said below
- coarse_live: int32 [4096, 128], P('dom'), may hold values 0 or 1
- coarse_bound: int32 [256, 128], P('dom'), may hold values from 0 to 1023
- edge_in: bfloat16 [3, 3, 128, 128], replicated, may hold values from -0.5 to 0.5
- edge_out: bfloat16 [3, 128, 128], replicated, may hold values from -0.5 to 0.5
- node_in: bfloat16 [3, 256, 128], replicated, may hold values from -0.375 to 0.375
- node_out: bfloat16 [3, 128, 128], replicated, may hold values from -0.5 to 0.5
Outputs:
- latents_out: bfloat16 [262144, 128], P('dom')
The draws below stay inside these ranges and needn't reach their ends.
Inputs may be any that keep to these rules, and one draw needn't show every extreme that they name: `coarse_send`: each coarse slot's sender lies in the lookup of its partition.
All inputs are finite; a program needn't handle non-finite values. No bound on the sum of `fine_live` or of `coarse_live` on one device may be relied on, other than what follows from the above.
Results may differ from the reference program's by a relative error of at most 0.015.
Values may be sent and summed in bfloat16 or wider, within the bound.
A program may use at most 64 MiB of HBM per device.

```python
import jax
import jax.numpy as jnp
from jax import lax

F = 128
HID = 128
NODES_DEV = 1024
LAYERS = 3
HALO = 256
CN_DEV = 256
CHALO = 64
TILES_DEV = 64
CTILES_DEV = 16
NODES = 262144
FINE_EDGES = 2097152
COARSE_EDGES = 524288
N_DOM = 256


def draw_coarse_send(key, part):
    key = jax.random.fold_in(key, 11)
    key_pick = jax.random.fold_in(key, 1)
    key_own = jax.random.fold_in(key, 2)
    key_rim = jax.random.fold_in(key, 3)
    shape = (N_DOM * CTILES_DEV, 128)
    picked = jax.random.randint(key_pick, shape, 0, 2, dtype=jnp.int32)
    own_index = jax.random.randint(key_own, shape, 0, NODES_DEV, dtype=jnp.int32)
    rim_index = jax.random.randint(key_rim, shape, NODES_DEV, NODES_DEV + 2 * CHALO, dtype=jnp.int32)
    result = jnp.where(picked == 0, own_index, rim_index)
    result = result.at[0, 0].set(0)
    result = result.at[-1, -1].set(NODES_DEV + 2 * CHALO - 1)
    return result.astype(jnp.int32)


def plant(drawn, key, smallest, largest):
    extent = drawn.shape
    spot = [jax.random.randint(jax.random.fold_in(key, axis), (), 0, extent[axis]) for axis in range(len(extent))]
    drawn = drawn.at[tuple(spot)].set(smallest)
    longest = extent.index(max(extent))
    spot[longest] = (spot[longest] + 1) % extent[longest]
    return drawn.at[tuple(spot)].set(largest)


def block_levels(stream_key, shape, shards, least, high):
    level = 1.0
    for position, parts in shards:
        steps = jax.random.uniform(jax.random.fold_in(jax.random.fold_in(stream_key, 6), position), (parts,), jnp.float32, least / len(shards), high / len(shards))
        level = level * jnp.repeat(jnp.exp(steps), shape[position] // parts).reshape((-1,) + (1,) * (len(shape) - 1 - position))
    return level


def centred(own_key, extent, scale, most, shards=(), held_as=jnp.bfloat16):
    drawn = scale * jax.random.normal(own_key, extent, jnp.float32)
    if shards:
        drawn = drawn * block_levels(own_key, extent, shards, -0.22, 0.18)
    return jnp.clip(drawn, -most, most).astype(held_as)


def setup_inputs(seed: int = 0) -> dict:
    seeds = jax.random.split(jax.random.key(seed), 17)
    nodes = centred(seeds[0], (NODES, F), 1.0, 6.0, ((0, 256),))
    fine_edges = centred(seeds[1], (FINE_EDGES, F), 1.0, 6.0, ((0, 256),))
    fine_recv = plant(jax.random.randint(seeds[2], (N_DOM * TILES_DEV, 128), 0, 128), jax.random.fold_in(seeds[2], 1), 0, 127).astype(jnp.int32)
    fine_send = plant(jax.random.randint(seeds[3], (N_DOM * TILES_DEV, 128), 0, NODES_DEV + 2 * HALO), jax.random.fold_in(seeds[3], 1), 0, (NODES_DEV + 2 * HALO) - 1).astype(jnp.int32)
    fine_live = plant((jax.random.randint(seeds[4], (N_DOM * TILES_DEV, 128), 0, 4) < 3).astype(jnp.int32), jax.random.fold_in(seeds[4], 1), 0, 1)
    bound_rows = plant(jax.random.randint(seeds[5], (N_DOM, 2 * HALO), 0, NODES_DEV), jax.random.fold_in(seeds[5], 1), 0, NODES_DEV - 1).astype(jnp.int32)
    cluster = plant(jax.random.randint(seeds[6], (NODES,), 0, NODES_DEV), jax.random.fold_in(seeds[6], 1), 0, NODES_DEV - 1).astype(jnp.int32)
    coarse_edges = centred(seeds[7], (COARSE_EDGES, F), 1.0, 6.0, ((0, 256),))
    coarse_recv = plant(jax.random.randint(seeds[8], (N_DOM * CTILES_DEV, 128), 0, 128), jax.random.fold_in(seeds[8], 1), 0, 127).astype(jnp.int32)
    coarse_send = draw_coarse_send(jax.random.fold_in(seeds[16], 71), 0)
    coarse_live = plant((jax.random.randint(seeds[10], (N_DOM * CTILES_DEV, 128), 0, 4) < 3).astype(jnp.int32), jax.random.fold_in(seeds[10], 1), 0, 1)
    coarse_bound = plant(jax.random.randint(seeds[11], (N_DOM, 2 * CHALO), 0, NODES_DEV), jax.random.fold_in(seeds[11], 1), 0, NODES_DEV - 1).astype(jnp.int32)
    edge_in = centred(seeds[12], (LAYERS, 3, F, HID), F ** -0.5, 0.5)
    edge_out = centred(seeds[13], (LAYERS, HID, F), HID ** -0.5, 0.5)
    node_in = centred(seeds[14], (LAYERS, 2 * F, HID), (2 * F) ** -0.5, 0.375)
    node_out = centred(seeds[15], (LAYERS, HID, F), HID ** -0.5, 0.5)
    return dict(nodes=nodes, fine_edges=fine_edges, fine_recv=fine_recv, fine_send=fine_send, fine_live=fine_live, bound_rows=bound_rows, cluster=cluster, coarse_edges=coarse_edges, coarse_recv=coarse_recv, coarse_send=coarse_send, coarse_live=coarse_live, coarse_bound=coarse_bound, edge_in=edge_in, edge_out=edge_out, node_in=node_in, node_out=node_out)


def layer_norm(values):
    center = lax.optimization_barrier(jnp.mean(values, axis=-1, keepdims=True))
    spread = lax.optimization_barrier(jnp.mean(jnp.square(values - center), axis=-1, keepdims=True))
    return (values - center) * lax.rsqrt(spread + 1e-05)

def process(own_nodes, lookup, edge_latent, receiver_slot, sender, live_mask, w_edge, w_message, w_node, w_update):
    tile_count = receiver_slot.shape[0]
    per_block = tile_count // (own_nodes.shape[0] // 128)
    block_start = (jnp.arange(tile_count, dtype=jnp.int32) // per_block * 128).astype(jnp.int32)
    target = (block_start[:, None] + receiver_slot).reshape(-1)
    from_recv = jnp.dot(own_nodes, w_edge[0], preferred_element_type=jnp.float32)
    from_send = jnp.dot(lookup, w_edge[1], preferred_element_type=jnp.float32)
    from_edge = jnp.dot(edge_latent, w_edge[2], preferred_element_type=jnp.float32)
    summed = from_recv[target] + from_send[sender.reshape(-1)] + from_edge
    active = jnp.maximum(summed, 0.0).astype(jnp.bfloat16)
    message = layer_norm(jnp.dot(active, w_message, preferred_element_type=jnp.float32)).astype(jnp.bfloat16)
    new_edges = (edge_latent.astype(jnp.float32) + message.astype(jnp.float32)).astype(jnp.bfloat16)
    slots = jnp.arange(128, dtype=jnp.int32)
    selector = ((receiver_slot[:, :, None] == slots[None, None, :]) & (live_mask[:, :, None] == 1)).astype(jnp.float32)
    per_tile = jnp.einsum('ten,tef->tnf', selector, message.astype(jnp.float32).reshape(tile_count, 128, -1))
    width = per_tile.shape[-1]
    aggregate = per_tile.reshape(-1, per_block, 128, width).sum(axis=1).reshape(own_nodes.shape[0], width)
    joined = jnp.concatenate([own_nodes, aggregate.astype(jnp.bfloat16)], axis=1)
    hidden = jnp.maximum(jnp.dot(joined, w_node, preferred_element_type=jnp.float32), 0.0).astype(jnp.bfloat16)
    updated = (own_nodes.astype(jnp.float32) + layer_norm(jnp.dot(hidden, w_update, preferred_element_type=jnp.float32))).astype(jnp.bfloat16)
    return (updated, new_edges)

def reference(nodes, fine_edges, fine_recv, fine_send, fine_live, bound_rows, cluster, coarse_edges, coarse_recv, coarse_send, coarse_live, coarse_bound, edge_in, edge_out, node_in, node_out):
    device_total = N_DOM
    groups = device_total // 4
    node_state = nodes.reshape(device_total, NODES_DEV, F)
    edge_state = fine_edges.reshape(device_total, TILES_DEV * 128, F)
    recv_tiles = fine_recv.reshape(device_total, TILES_DEV, 128)
    send_tiles = fine_send.reshape(device_total, TILES_DEV, 128)
    live_tiles = fine_live.reshape(device_total, TILES_DEV, 128)

    def take_rows(node_block, picked_rows):
        return node_block[picked_rows]

    def fine_layer(node_state, edge_state, layer_index):
        outgoing = jax.vmap(take_rows)(node_state, bound_rows)
        from_left = jnp.roll(outgoing[:, HALO:], 1, axis=0)
        from_right = jnp.roll(outgoing[:, :HALO], -1, axis=0)
        lookup = jnp.concatenate([node_state, from_left, from_right], axis=1)

        def single(inputs):
            return process(*inputs, edge_in[layer_index], edge_out[layer_index], node_in[layer_index], node_out[layer_index])
        return lax.map(single, (node_state, lookup, edge_state, recv_tiles, send_tiles, live_tiles))
    node_state, edge_state = fine_layer(node_state, edge_state, 0)
    grouped = node_state.reshape(groups, 4 * NODES_DEV, F).astype(jnp.float32)
    members = cluster.reshape(groups, 4 * NODES_DEV)

    def pool_sum(node_block, labels):
        return jax.ops.segment_sum(node_block, labels, num_segments=NODES_DEV)

    def pool_count(labels):
        return jax.ops.segment_sum(jnp.ones(labels.shape, jnp.float32), labels, num_segments=NODES_DEV)
    cluster_sums = jax.vmap(pool_sum)(grouped, members)
    counts = jax.vmap(pool_count)(members)
    coarse = (cluster_sums / jnp.maximum(counts, 1.0)[:, :, None]).astype(jnp.bfloat16)
    repeated = jnp.repeat(coarse, 4, axis=0)
    coarse_out = jax.vmap(take_rows)(repeated, coarse_bound)
    coarse_from_left = jnp.roll(coarse_out[:, CHALO:], 4, axis=0)
    coarse_from_right = jnp.roll(coarse_out[:, :CHALO], -4, axis=0)
    coarse_lookup = jnp.concatenate([repeated, coarse_from_left, coarse_from_right], axis=1)
    quarters = coarse.reshape(device_total, CN_DEV, F)

    def coarse_single(inputs):
        return process(*inputs, edge_in[1], edge_out[1], node_in[1], node_out[1])
    new_quarters, unused = lax.map(coarse_single, (quarters, coarse_lookup, coarse_edges.reshape(device_total, CTILES_DEV * 128, F), coarse_recv.reshape(device_total, CTILES_DEV, 128), coarse_send.reshape(device_total, CTILES_DEV, 128), coarse_live.reshape(device_total, CTILES_DEV, 128)))
    coarse_new = new_quarters.reshape(groups, NODES_DEV, F)
    lifted = jax.vmap(take_rows)(coarse_new, members)
    node_state = (node_state.reshape(groups, 4 * NODES_DEV, F).astype(jnp.float32) + lifted.astype(jnp.float32)).astype(jnp.bfloat16)
    node_state = node_state.reshape(device_total, NODES_DEV, F)
    final_state, unused = fine_layer(node_state, edge_state, 2)
    return final_state.reshape(device_total * NODES_DEV, F)
```

```python
import functools

import jax
import jax.numpy as jnp
from jax import lax
from jax.experimental import pallas as pl
from jax.experimental.pallas import tpu as pltpu
from jax.sharding import PartitionSpec as P

MESH = pl.DeviceIdType.MESH
BF = jnp.bfloat16
F32 = jnp.float32
I32 = jnp.int32
SLOTS = 1024


def dot(a, b):
    return jnp.dot(a, b, preferred_element_type=F32)


def dot_nt(a, b):
    return lax.dot_general(a, b, (((1,), (1,)), ((), ())), preferred_element_type=F32)


def onehot(index, rows):
    numbers = lax.broadcasted_iota(jnp.int16, (rows, index.shape[1]), 0)
    return jnp.where(numbers == index.astype(jnp.int16), jnp.ones((), BF), jnp.zeros((), BF))


def half_of(upper, folded):
    return jnp.where(upper == 1, folded[128:], folded[:128])


def centred(weight_t):
    wide = weight_t.astype(F32)
    return (wide - jnp.mean(wide, axis=0, keepdims=True)).astype(BF)


def normalised(values):
    spread = jnp.mean(values * values, axis=0, keepdims=True)
    return values * lax.rsqrt(spread + 1e-05)


def index_row(ref, tile, tiles):
    base = pl.multiple_of(tile, 8)
    rows = ref[pl.ds(base, 8), :]
    return jnp.concatenate([rows[i : i + 1, :] for i in range(tiles)], axis=1)


def kernel(
    total,
    nodes_h,
    fine_edges_h,
    fine_recv_h,
    fine_send_h,
    fine_live_h,
    bound_h,
    cluster_h,
    coarse_edges_h,
    coarse_recv_h,
    coarse_send_h,
    coarse_live_h,
    coarse_bound_h,
    edge_in_h,
    edge_out_h,
    node_in_h,
    node_out_h,
    out_ref,
    nodes,
    fine_edges,
    fine_recv,
    fine_send,
    fine_live,
    bound,
    cluster,
    coarse_edges,
    coarse_recv,
    coarse_send,
    coarse_live,
    coarse_bound,
    edge_in,
    edge_out,
    node_in,
    node_out,
    state,
    edges_t,
    before,
    aggregate,
    recv_table,
    own_table,
    halo_table,
    halo_out,
    cluster_hot,
    count_out,
    count_in,
    part,
    part_in,
    pair_out,
    pair_in,
    coarse_table,
    coarse_out,
    coarse_in,
    coarse_new,
    load_sem,
    edge_sem,
    send_sem,
    recv_sem,
):
    me = lax.axis_index("dom")
    q = lax.rem(me, 4)
    base = me - q
    parity = lax.rem(q, 2)
    half = q // 2
    left = lax.rem(me + total - 1, total)
    right = lax.rem(me + 1, total)
    down = lax.rem(me + total - 4, total)
    up = lax.rem(me + 4, total)
    mate = [None, base + q + 1 - 2 * parity, base + q + 2 - 4 * half, base + 3 - q]

    def remote(slot, src, dst, device):
        return pltpu.make_async_remote_copy(
            src_ref=src,
            dst_ref=dst,
            send_sem=send_sem.at[slot],
            recv_sem=recv_sem.at[slot],
            device_id=(device,),
            device_id_type=MESH,
        )

    barrier = pltpu.get_barrier_semaphore()
    for other in (left, right, down, up, mate[1], mate[2], mate[3]):
        pl.semaphore_signal(barrier, inc=1, device_id=(other,), device_id_type=MESH)

    loads = {}
    for i, (name, src, dst) in enumerate(
        (
            ("nodes", nodes_h, nodes),
            ("edge_in", edge_in_h, edge_in),
            ("bound", bound_h, bound),
            ("fine_send", fine_send_h, fine_send),
            ("fine_recv", fine_recv_h, fine_recv),
            ("cluster", cluster_h, cluster),
            ("fine_live", fine_live_h, fine_live),
            ("edge_out", edge_out_h, edge_out),
            ("node_in", node_in_h, node_in),
            ("node_out", node_out_h, node_out),
            ("coarse_edges", coarse_edges_h, coarse_edges),
            ("coarse_recv", coarse_recv_h, coarse_recv),
            ("coarse_send", coarse_send_h, coarse_send),
            ("coarse_live", coarse_live_h, coarse_live),
            ("coarse_bound", coarse_bound_h, coarse_bound),
        )
    ):
        loads[name] = pltpu.make_async_copy(src, dst, load_sem.at[i])

    def edge_load(b):
        rows = pl.ds(pl.multiple_of(b * 1024, 1024), 1024)
        return pltpu.make_async_copy(fine_edges_h.at[rows], fine_edges.at[rows], edge_sem.at[b])

    for name in ("nodes", "edge_in", "bound", "fine_send", "fine_recv", "cluster"):
        loads[name].start()
    for b in range(8):
        edge_load(b).start()
    for name in loads:
        if name not in ("nodes", "edge_in", "bound", "fine_send", "fine_recv", "cluster"):
            loads[name].start()

    def own_part(layer, blocks, recv_ref, send_ref, edge_block):
        w_edge = edge_in[layer, 2].T

        def block(b, carry):
            send = index_row(send_ref, b * 8, 8)
            recv = index_row(recv_ref, b * 8, 8)
            inside = jnp.where(send < 1024, send & 511, -1)
            gathered = half_of((send >> 9) & 1, dot(own_table[...], onehot(inside, 512)))
            joined = jnp.concatenate([recv_table[b], w_edge], axis=1)
            columns = jnp.concatenate([onehot(recv, 128), edge_block(b)], axis=0)
            before[:, pl.ds(pl.multiple_of(b * 1024, 1024), 1024)] = gathered + dot(joined, columns)
            return carry

        lax.fori_loop(0, blocks, block, 0)

    def messages(layer, blocks, recv_ref, live_ref, rim_part, keep):
        w_message = centred(edge_out[layer].T)

        def block(b, carry):
            columns = pl.ds(pl.multiple_of(b * 1024, 1024), 1024)
            summed = before[:, columns] + rim_part(b)
            active = jnp.maximum(summed, 0.0).astype(BF)
            message = normalised(dot(w_message, active)).astype(BF)
            if keep:
                edges_t[:, columns] = (
                    edges_t[:, columns].astype(F32) + message.astype(F32)
                ).astype(BF)
            target = jnp.where(index_row(live_ref, b * 8, 8) == 1, index_row(recv_ref, b * 8, 8), -1)
            aggregate[b] = dot_nt(message, onehot(target, 128))
            return carry

        lax.fori_loop(0, blocks, block, 0)

    def node_update(layer, blocks, own):
        totals = jnp.concatenate([aggregate[b] for b in range(blocks)], axis=1)
        joined = jnp.concatenate([own, totals.astype(BF)], axis=0)
        hidden = jnp.maximum(dot(node_in[layer].T, joined), 0.0).astype(BF)
        change = normalised(dot(centred(node_out[layer].T), hidden))
        return (own.astype(F32) + change).astype(BF)

    def fine_tables(layer):
        own = state[...]
        table = dot(edge_in[layer, 1].T, own).astype(BF)
        own_table[:128, :] = table[:, :512]
        own_table[128:, :] = table[:, 512:]

    def recv_tables(layer, own, blocks):
        table = dot(edge_in[layer, 0].T, own).astype(BF)
        for b in range(blocks):
            recv_table[b] = table[:, b * 128 : (b + 1) * 128]

    def fine_halo(which):
        rows = bound[...]
        picked = half_of(rows >> 9, dot(own_table[...], onehot(rows & 511, 512))).astype(BF)
        halo_out[which, 0] = picked[:, :256]
        halo_out[which, 1] = picked[:, 256:]
        to_left = remote(
            2 * which,
            halo_out.at[which, 0],
            halo_table.at[which, pl.ds(128, 128)],
            left,
        )
        to_right = remote(
            2 * which + 1,
            halo_out.at[which, 1],
            halo_table.at[which, pl.ds(0, 128)],
            right,
        )
        return to_left, to_right

    def fine_rim(which):
        def rim_part(b):
            send = index_row(fine_send, b * 8, 8)
            outside = jnp.where(send >= 1024, send & 255, -1)
            return half_of((send >> 8) & 1, dot(halo_table[which], onehot(outside, 256)))

        return rim_part

    loads["nodes"].wait()
    loads["edge_in"].wait()
    loads["bound"].wait()
    state[...] = nodes[...].T
    fine_tables(0)
    copies = fine_halo(0)
    pl.semaphore_wait(barrier, 7)
    for copy in copies:
        copy.start()

    loads["cluster"].wait()
    label = index_row(cluster, 0, 8)
    cluster_hot[...] = onehot(label & 511, 512)
    members = lax.broadcasted_iota(I32, (16, 1024), 0) // 8 == (label >> 9)
    count_out[...] = dot_nt(jnp.where(members, 1.0, 0.0).astype(BF), cluster_hot[...])
    count_copies = [remote(3 + k, count_out, count_in.at[k - 1], mate[k]) for k in (1, 2, 3)]
    for copy in count_copies:
        copy.start()

    recv_tables(0, state[...], 8)
    loads["fine_send"].wait()
    loads["fine_recv"].wait()

    def first_edges(b):
        edge_load(b).wait()
        turned = fine_edges[pl.ds(pl.multiple_of(b * 1024, 1024), 1024), :].T
        edges_t[:, pl.ds(pl.multiple_of(b * 1024, 1024), 1024)] = turned
        return turned

    own_part(0, 8, fine_recv, fine_send, first_edges)
    loads["edge_out"].wait()
    loads["fine_live"].wait()
    for copy in copies:
        copy.wait()
    messages(0, 8, fine_recv, fine_live, fine_rim(0), True)
    loads["node_in"].wait()
    loads["node_out"].wait()
    state[...] = node_update(0, 8, state[...])

    for copy in count_copies:
        copy.wait()
    counts = count_out[...] + count_in[0] + count_in[1] + count_in[2]
    share = 1.0 / jnp.maximum(counts, 1.0)
    fine = state[...]
    nothing = jnp.zeros_like(fine)
    folded = jnp.concatenate(
        [jnp.where(label < 512, fine, nothing), jnp.where(label < 512, nothing, fine)], axis=0
    )
    sums = dot_nt(folded, cluster_hot[...])
    for i in range(2):
        means = (sums[i * 128 : i * 128 + 128] * share[i * 8 : i * 8 + 1]).astype(BF)
        part[0, i] = means[:, :256]
        part[1, i] = means[:, 256:]
    copy = remote(7, part.at[1 - parity], part_in, mate[1])
    copy.start()
    copy.wait()
    pair_out[...] = (part[parity].astype(F32) + part_in[...].astype(F32)).astype(BF)
    copy = remote(8, pair_out.at[1 - half], pair_in, mate[2])
    copy.start()
    copy.wait()
    quarter = (pair_out[half].astype(F32) + pair_in[...].astype(F32)).astype(BF)

    coarse_table[parity, half] = dot(edge_in[1, 1].T, quarter).astype(BF)
    copy = remote(9, coarse_table.at[parity, half], coarse_table.at[parity, half], mate[2])
    copy.start()
    recv_tables(1, quarter, 2)
    for name in ("coarse_edges", "coarse_recv", "coarse_send", "coarse_live", "coarse_bound"):
        loads[name].wait()
    copy.wait()
    copy = remote(10, coarse_table.at[parity], coarse_table.at[parity], mate[1])
    copy.start()
    copy.wait()
    for i in range(2):
        own_table[:, i * 256 : i * 256 + 256] = coarse_table[i].reshape(256, 256)
    rows = coarse_bound[...]
    coarse_out[...] = half_of(rows >> 9, dot(own_table[...], onehot(rows & 511, 512))).astype(BF)
    copies = (
        remote(11, coarse_out, coarse_in.at[1], down),
        remote(12, coarse_out, coarse_in.at[0], up),
    )
    for copy in copies:
        copy.start()

    def coarse_block(b):
        return coarse_edges[pl.ds(pl.multiple_of(b * 1024, 1024), 1024), :].T

    own_part(1, 2, coarse_recv, coarse_send, coarse_block)
    for copy in copies:
        copy.wait()
    lane = lax.broadcasted_iota(I32, (128, 128), 1)
    rim = jnp.where(lane < 64, coarse_in[1].astype(F32), coarse_in[0].astype(F32)).astype(BF)

    def coarse_rim(b):
        send = index_row(coarse_send, b * 8, 8)
        place = jnp.where(send < 1088, (send & 63) + 64, send & 63)
        return dot(rim, onehot(jnp.where(send >= 1024, place, -1), 128))

    messages(1, 2, coarse_recv, coarse_live, coarse_rim, False)
    coarse_new[parity, half] = node_update(1, 2, quarter)
    copy = remote(13, coarse_new.at[parity, half], coarse_new.at[parity, half], mate[2])
    copy.start()
    copy.wait()
    copy = remote(14, coarse_new.at[parity], coarse_new.at[parity], mate[1])
    copy.start()
    copy.wait()
    lifted = dot(coarse_new[0].reshape(256, 256), cluster_hot[:256, :])
    lifted += dot(coarse_new[1].reshape(256, 256), cluster_hot[256:, :])
    state[...] = (state[...].astype(F32) + half_of(label >> 9, lifted)).astype(BF)

    fine_tables(2)
    copies = fine_halo(1)
    for copy in copies:
        copy.start()
    recv_tables(2, state[...], 8)

    def last_edges(b):
        return edges_t[:, pl.ds(pl.multiple_of(b * 1024, 1024), 1024)]

    own_part(2, 8, fine_recv, fine_send, last_edges)
    for copy in copies:
        copy.wait()
    messages(2, 8, fine_recv, fine_live, fine_rim(1), False)
    out_ref[...] = node_update(2, 8, state[...]).T


def local(
    nodes,
    fine_edges,
    fine_recv,
    fine_send,
    fine_live,
    bound_rows,
    cluster,
    coarse_edges,
    coarse_recv,
    coarse_send,
    coarse_live,
    coarse_bound,
    edge_in,
    edge_out,
    node_in,
    node_out,
):
    args = (
        nodes,
        fine_edges,
        fine_recv,
        fine_send,
        fine_live,
        bound_rows,
        cluster.reshape(8, 128),
        coarse_edges,
        coarse_recv,
        coarse_send,
        coarse_live,
        coarse_bound,
        edge_in,
        edge_out,
        node_in,
        node_out,
    )
    vmem = pltpu.VMEM
    return pl.pallas_call(
        functools.partial(kernel, lax.axis_size("dom")),
        out_shape=jax.ShapeDtypeStruct((1024, 128), BF),
        in_specs=[pl.BlockSpec(memory_space=pl.ANY)] * len(args),
        out_specs=pl.BlockSpec(memory_space=pltpu.VMEM),
        scratch_shapes=[vmem(a.shape, a.dtype) for a in args]
        + [
            vmem((128, 1024), BF),
            vmem((128, 8192), BF),
            vmem((128, 8192), F32),
            vmem((8, 128, 128), F32),
            vmem((8, 128, 128), BF),
            vmem((256, 512), BF),
            vmem((2, 256, 256), BF),
            vmem((2, 2, 128, 256), BF),
            vmem((512, 1024), BF),
            vmem((16, 512), F32),
            vmem((3, 16, 512), F32),
            vmem((2, 2, 128, 256), BF),
            vmem((2, 128, 256), BF),
            vmem((2, 128, 256), BF),
            vmem((128, 256), BF),
            vmem((2, 2, 128, 256), BF),
            vmem((128, 128), BF),
            vmem((2, 128, 128), BF),
            vmem((2, 2, 128, 256), BF),
            pltpu.SemaphoreType.DMA((15,)),
            pltpu.SemaphoreType.DMA((8,)),
            pltpu.SemaphoreType.DMA((15,)),
            pltpu.SemaphoreType.DMA((15,)),
        ],
        compiler_params=pltpu.CompilerParams(
            collective_id=0, has_side_effects=True, vmem_limit_bytes=56 << 20
        ),
    )(*args)


def solution(mesh):
    row = P("dom", None)
    return jax.shard_map(
        local,
        mesh=mesh,
        in_specs=(row,) * 6 + (P("dom"),) + (row,) * 5 + (P(),) * 4,
        out_specs=row,
        check_vma=False,
    )
```

```python
import functools

import jax
import jax.numpy as jnp
from jax import lax
from jax.experimental import pallas as pl
from jax.experimental.pallas import tpu as pltpu
from jax.sharding import PartitionSpec as P

MESH = pl.DeviceIdType.MESH
BF = jnp.bfloat16
F32 = jnp.float32
I32 = jnp.int32


def dot(a, b):
    return jnp.dot(a, b, preferred_element_type=F32)


def dot_nt(a, b):
    return lax.dot_general(a, b, (((1,), (1,)), ((), ())), preferred_element_type=F32)


def onehot(index, rows):
    numbers = lax.broadcasted_iota(jnp.int16, (rows, index.shape[1]), 0)
    return jnp.where(numbers == index.astype(jnp.int16), jnp.ones((), BF), jnp.zeros((), BF))


def half_of(upper, folded):
    return jnp.where(upper == 1, folded[128:], folded[:128])


def centred(weight_t):
    wide = weight_t.astype(F32)
    return (wide - jnp.mean(wide, axis=0, keepdims=True)).astype(BF)


def normalised(values):
    spread = jnp.mean(values * values, axis=0, keepdims=True)
    return values * lax.rsqrt(spread + 1e-05)


def index_row(ref, block):
    rows = ref[block * 8 : block * 8 + 8, :]
    return jnp.concatenate([rows[i : i + 1, :] for i in range(8)], axis=1)


def block_lanes(block):
    return slice(block * 1024, block * 1024 + 1024)


INPUTS = (
    "nodes",
    "edge_in",
    "bound",
    "cluster",
    "fine_send",
    "fine_recv",
    "fine_edges",
    "coarse_bound",
    "edge_out",
    "fine_live",
    "node_in",
    "node_out",
    "coarse_edges",
    "coarse_recv",
    "coarse_send",
    "coarse_live",
)
SCRATCH = dict(
    state=((128, 1024), BF),
    edges_t=((128, 8192), BF),
    before=((128, 8192), F32),
    aggregate=((8, 128, 128), F32),
    recv_table=((8, 128, 128), BF),
    own_table=((256, 512), BF),
    bound_hot=((512, 512), BF),
    cluster_hot=((512, 1024), BF),
    halo_out=((2, 128, 256), BF),
    halo_in=((256, 256), BF),
    later_out=((2, 128, 256), BF),
    later_in=((2, 128, 256), BF),
    near_out=((2, 8, 256), I32),
    near_in=((2, 8, 256), I32),
    list_in=((1, 128), I32),
    count_out=((16, 512), F32),
    count_in=((3, 16, 512), F32),
    part=((2, 256, 256), BF),
    part_in=((2, 256, 256), BF),
    chip=((2, 256, 256), BF),
    chip_in=((256, 256), BF),
    mine=((2, 128, 256), BF),
    coarse_table=((2, 256, 256), BF),
    rim_out=((4, 64, 128), BF),
    rim_in=((2, 2, 64, 128), BF),
    fresh=((3, 2, 2, 128, 256), BF),
)
COPIES = (
    ["halo_l", "halo_r", "near_l", "near_r", "later_l", "later_r", "list"]
    + ["count1", "count2", "count3", "pool1", "pool2", "table"]
    + ["rim0", "rim1", "rim2", "rim3", "fresh2", "fresh1"]
    + ["ahead0", "ahead1", "ahead2", "ahead3", "back0", "back1", "back2", "back3"]
)


class Refs:
    pass


def kernel(total, *refs):
    hbm = dict(zip(INPUTS, refs))
    out_ref = refs[len(INPUTS)]
    r = Refs()
    for name, ref in zip(INPUTS + tuple(SCRATCH), refs[len(INPUTS) + 1 :]):
        setattr(r, name, ref)
    load_sem, edge_sem, send_sem, recv_sem = refs[-4:]

    me = lax.axis_index("dom")
    q = lax.rem(me, 4)
    base = me - q
    parity = lax.rem(q, 2)
    half = q // 2
    left = lax.rem(me + total - 1, total)
    right = lax.rem(me + 1, total)
    down = lax.rem(me + total - 4, total)
    up = lax.rem(me + 4, total)
    mate1 = base + q + 1 - 2 * parity
    mate2 = base + q + 2 - 4 * half
    mate3 = base + 3 - q
    mate2_down = lax.rem(mate2 + total - 4, total)
    mate2_up = lax.rem(mate2 + 4, total)
    ahead = lax.rem(base + 4, total)
    back = lax.rem(base + total - 1, total)

    def remote(name, src, dst, device, arrives=None):
        slot = COPIES.index(name)
        return pltpu.make_async_remote_copy(
            src_ref=src,
            dst_ref=dst,
            send_sem=send_sem.at[slot],
            recv_sem=recv_sem.at[slot if arrives is None else arrives],
            device_id=(device,),
            device_id_type=MESH,
        )

    barrier = pltpu.get_barrier_semaphore()

    def greet(device):
        pl.semaphore_signal(barrier, inc=1, device_id=(device,), device_id_type=MESH)

    loads = {}
    for i, name in enumerate(INPUTS):
        if name != "fine_edges":
            loads[name] = pltpu.make_async_copy(hbm[name], getattr(r, name), load_sem.at[i])

    def edge_load(b):
        rows = pl.ds(b * 1024, 1024)
        return pltpu.make_async_copy(
            hbm["fine_edges"].at[rows], r.fine_edges.at[rows], edge_sem.at[b]
        )

    loads["nodes"].start()
    loads["edge_in"].start()
    loads["bound"].start()
    loads["cluster"].start()
    for device in (left, right, mate1, mate2, mate3, down, up, mate2_down, mate2_up):
        greet(device)

    @pl.when(q == 0)
    def _():
        for i in range(4):
            greet(lax.rem(base + total - 4 + i, total))

    @pl.when(q == 3)
    def _():
        for i in range(4):
            greet(lax.rem(base + 4 + i, total))

    for name in INPUTS[4:]:
        if name == "fine_edges":
            for b in range(8):
                edge_load(b).start()
        else:
            loads[name].start()

    def own_part(layer, blocks, recv_ref, send_ref, table, edge_block):
        w_edge = r.edge_in[layer, 2].T
        for b in range(blocks):
            send = index_row(send_ref, b)
            inside = jnp.where(send < 1024, send & 511, -1)
            gathered = half_of((send >> 9) & 1, dot(table, onehot(inside, 512)))
            joined = jnp.concatenate([r.recv_table[b], w_edge], axis=1)
            columns = jnp.concatenate([onehot(index_row(recv_ref, b), 128), edge_block(b)], axis=0)
            r.before[:, block_lanes(b)] = gathered + dot(joined, columns)

    def fine_rim():
        for b in range(8):
            send = index_row(r.fine_send, b)
            outside = jnp.where(send >= 1024, send & 255, -1)
            r.before[:, block_lanes(b)] += half_of(
                (send >> 8) & 1, dot(r.halo_in[...], onehot(outside, 256))
            )

    def messages(layer, blocks, recv_ref, live_ref, keep):
        w_message = centred(r.edge_out[layer].T)
        for b in range(blocks):
            lanes = block_lanes(b)
            active = jnp.maximum(r.before[:, lanes], 0.0).astype(BF)
            message = normalised(dot(w_message, active)).astype(BF)
            if keep:
                r.edges_t[:, lanes] = (
                    r.edges_t[:, lanes].astype(F32) + message.astype(F32)
                ).astype(BF)
            target = jnp.where(index_row(live_ref, b) == 1, index_row(recv_ref, b), -1)
            r.aggregate[b] = dot_nt(message, onehot(target, 128))

    def node_update(layer, blocks, own):
        totals = jnp.concatenate([r.aggregate[b] for b in range(blocks)], axis=1)
        joined = jnp.concatenate([own, totals.astype(BF)], axis=0)
        hidden = jnp.maximum(dot(r.node_in[layer].T, joined), 0.0).astype(BF)
        change = normalised(dot(centred(r.node_out[layer].T), hidden))
        return (own.astype(F32) + change).astype(BF)

    def fine_tables(layer, own):
        table = dot(r.edge_in[layer, 1].T, own).astype(BF)
        r.own_table[:128, :] = table[:, :512]
        r.own_table[128:, :] = table[:, 512:]

    def recv_tables(layer, own, blocks):
        table = dot(r.edge_in[layer, 0].T, own).astype(BF)
        for b in range(blocks):
            r.recv_table[b] = table[:, b * 128 : (b + 1) * 128]

    def lift(group, index):
        hot = onehot(index & 511, 512)
        found = dot(r.fresh[group, 0].reshape(256, 256), hot[:256])
        found += dot(r.fresh[group, 1].reshape(256, 256), hot[256:])
        return half_of(index >> 9, found)

    for name in ("nodes", "edge_in", "bound"):
        loads[name].wait()
    r.state[...] = r.nodes[...].T
    fine_tables(0, r.state[...])
    rows = r.bound[...]
    r.bound_hot[...] = onehot(rows & 511, 512)
    picked = half_of(rows >> 9, dot(r.own_table[...], r.bound_hot[...])).astype(BF)
    r.halo_out[0] = picked[:, :256]
    r.halo_out[1] = picked[:, 256:]
    halo = (
        remote("halo_l", r.halo_out.at[0], r.halo_in.at[pl.ds(128, 128)], left),
        remote("halo_r", r.halo_out.at[1], r.halo_in.at[pl.ds(0, 128)], right),
    )

    loads["cluster"].wait()
    label = index_row(r.cluster, 0)
    digits = []
    for columns in (label[:, :512], label[:, 512:]):
        for digit in (columns & 255, columns >> 8):
            digits.append(jnp.broadcast_to(digit.astype(F32), (8, 512)).astype(BF))
    found = dot(jnp.concatenate(digits, axis=0), r.bound_hot[...])
    upper = jnp.broadcast_to(rows >> 9, (8, 512)) == 1
    low = jnp.where(upper, found[16:24], found[0:8])
    high = jnp.where(upper, found[24:32], found[8:16])
    near = (low + 256.0 * high).astype(I32)
    r.near_out[0] = near[:, :256]
    r.near_out[1] = near[:, 256:]
    r.cluster_hot[...] = onehot(label & 511, 512)
    members = lax.broadcasted_iota(I32, (16, 1024), 0) // 8 == (label >> 9)
    r.count_out[...] = dot_nt(jnp.where(members, 1.0, 0.0).astype(BF), r.cluster_hot[...])
    recv_tables(0, r.state[...], 8)
    loads["coarse_bound"].wait()

    pl.semaphore_wait(barrier, 11)
    early = halo + (
        remote("near_l", r.near_out.at[0], r.near_in.at[1], left),
        remote("near_r", r.near_out.at[1], r.near_in.at[0], right),
        remote("count1", r.count_out, r.count_in.at[0], mate1),
        remote("count2", r.count_out, r.count_in.at[1], mate2),
        remote("count3", r.count_out, r.count_in.at[2], mate3),
        remote("list", r.coarse_bound, r.list_in, mate2),
    )
    for copy in early:
        copy.start()

    loads["fine_send"].wait()
    loads["fine_recv"].wait()

    def first_edges(b):
        edge_load(b).wait()
        turned = r.fine_edges[pl.ds(b * 1024, 1024), :].T
        r.edges_t[:, block_lanes(b)] = turned
        return turned

    own_part(0, 8, r.fine_recv, r.fine_send, r.own_table[...], first_edges)
    for name in INPUTS[8:]:
        loads[name].wait()
    for copy in halo:
        copy.wait()
    fine_rim()
    messages(0, 8, r.fine_recv, r.fine_live, True)
    r.state[...] = node_update(0, 8, r.state[...])

    for copy in early[2:]:
        copy.wait()
    share = 1.0 / jnp.maximum(r.count_out[...] + r.count_in[0] + r.count_in[1] + r.count_in[2], 1.0)
    fine = r.state[...]
    nothing = jnp.zeros_like(fine)
    folded = jnp.concatenate(
        [jnp.where(label < 512, fine, nothing), jnp.where(label < 512, nothing, fine)], axis=0
    )
    sums = dot_nt(folded, r.cluster_hot[...])
    for i in range(2):
        means = (sums[i * 128 : i * 128 + 128] * share[i * 8 : i * 8 + 1]).astype(BF)
        for j in range(2):
            r.part[j, i * 128 : i * 128 + 128] = means[:, j * 256 : j * 256 + 256]
    copy = remote("pool1", r.part, r.part_in, mate1)
    copy.start()
    copy.wait()
    r.chip[...] = (r.part[...].astype(F32) + r.part_in[...].astype(F32)).astype(BF)
    pool = remote("pool2", r.chip.at[parity], r.chip_in, mate2)
    pool.start()

    rows = jnp.concatenate([r.coarse_bound[...], r.list_in[...]], axis=1)
    both = jnp.concatenate([r.chip[0], r.chip[1]], axis=1)
    picked = half_of(rows >> 9, dot(both, onehot(rows & 511, 512)))
    r.rim_out[...] = picked.T.astype(BF).reshape(4, 64, 128)
    rims = (
        remote("rim0", r.rim_out.at[0], r.rim_in.at[1, 0], down),
        remote("rim1", r.rim_out.at[1], r.rim_in.at[0, 0], up),
        remote("rim2", r.rim_out.at[2], r.rim_in.at[1, 1], mate2_down),
        remote("rim3", r.rim_out.at[3], r.rim_in.at[0, 1], mate2_up),
    )
    for copy in rims:
        copy.start()
    pool.wait()
    r.mine[...] = (
        (r.chip[parity].astype(F32) + r.chip_in[...].astype(F32)).astype(BF).reshape(2, 128, 256)
    )

    w_send = r.edge_in[1, 1].T
    for i in range(2):
        r.coarse_table[parity, i * 128 : i * 128 + 128] = dot(w_send, r.mine[i]).astype(BF)
    copy = remote("table", r.coarse_table.at[parity], r.coarse_table.at[parity], mate1)
    copy.start()
    quarter = r.mine[half]
    recv_tables(1, quarter, 2)

    table = jnp.concatenate([fine[:, :512], fine[:, 512:]], axis=0)
    picked = half_of(r.bound[...] >> 9, dot(table, r.bound_hot[...])).astype(BF)
    r.later_out[0] = picked[:, :256]
    r.later_out[1] = picked[:, 256:]
    later = (
        remote("later_l", r.later_out.at[0], r.later_in.at[1], left),
        remote("later_r", r.later_out.at[1], r.later_in.at[0], right),
    )
    copy.wait()
    for item in later:
        item.start()

    def coarse_block(b):
        return r.coarse_edges[pl.ds(b * 1024, 1024), :].T

    table = jnp.concatenate([r.coarse_table[0], r.coarse_table[1]], axis=1)
    own_part(1, 2, r.coarse_recv, r.coarse_send, table, coarse_block)
    for copy in rims:
        copy.wait()
    rim = (r.rim_in[:, 0].astype(F32) + r.rim_in[:, 1].astype(F32)).astype(BF).reshape(128, 128)
    rim_table = dot_nt(w_send, rim).astype(BF)
    for b in range(2):
        send = index_row(r.coarse_send, b)
        outside = jnp.where(send >= 1024, send & 127, -1)
        r.before[:, block_lanes(b)] += dot(rim_table, onehot(outside, 128))
    messages(1, 2, r.coarse_recv, r.coarse_live, False)

    r.fresh[1, parity, half] = node_update(1, 2, quarter)
    own = r.fresh.at[1, parity, half]
    sender = 2 * parity + half
    copy = remote("fresh2", own, own, mate2)
    copy.start()
    beside = (
        remote("ahead0", own, r.fresh.at[0, parity, half], ahead, COPIES.index("ahead0") + sender),
        remote("back0", own, r.fresh.at[2, parity, half], back, COPIES.index("back0") + sender),
    )
    for item in beside:
        item.start()
    copy.wait()
    copy = remote("fresh1", r.fresh.at[1, parity], r.fresh.at[1, parity], mate1)
    copy.start()
    copy.wait()
    r.state[...] = (r.state[...].astype(F32) + lift(1, label)).astype(BF)

    fine_tables(2, r.state[...])
    recv_tables(2, r.state[...], 8)
    own_part(
        2, 8, r.fine_recv, r.fine_send, r.own_table[...], lambda b: r.edges_t[:, block_lanes(b)]
    )
    for item in later:
        item.wait()
    for item in beside:
        item.wait_send()

    def arrive(name, group):
        for i in range(4):
            block = r.fresh.at[group, i // 2, i % 2]
            remote(name + str(i), block, block, left).wait_recv()

    @pl.when(q == 0)
    def _():
        arrive("ahead", 0)

    @pl.when(q == 3)
    def _():
        arrive("back", 2)

    w_send = r.edge_in[2, 1].T
    for side, group in ((0, jnp.where(q == 0, 0, 1)), (1, jnp.where(q == 3, 2, 1))):
        raised = lift(group, r.near_in[side][:1, :])
        rim = (r.later_in[side].astype(F32) + raised).astype(BF)
        r.halo_in[side * 128 : side * 128 + 128] = dot(w_send, rim).astype(BF)
    fine_rim()
    messages(2, 8, r.fine_recv, r.fine_live, False)
    out_ref[...] = node_update(2, 8, r.state[...]).T


def local(
    nodes,
    fine_edges,
    fine_recv,
    fine_send,
    fine_live,
    bound_rows,
    cluster,
    coarse_edges,
    coarse_recv,
    coarse_send,
    coarse_live,
    coarse_bound,
    edge_in,
    edge_out,
    node_in,
    node_out,
):
    args = dict(
        nodes=nodes,
        edge_in=edge_in,
        bound=bound_rows,
        cluster=cluster.reshape(8, 128),
        fine_send=fine_send,
        fine_recv=fine_recv,
        fine_edges=fine_edges,
        coarse_bound=coarse_bound,
        edge_out=edge_out,
        fine_live=fine_live,
        node_in=node_in,
        node_out=node_out,
        coarse_edges=coarse_edges,
        coarse_recv=coarse_recv,
        coarse_send=coarse_send,
        coarse_live=coarse_live,
    )
    held = [(args[name].shape, args[name].dtype) for name in INPUTS] + list(SCRATCH.values())
    return pl.pallas_call(
        functools.partial(kernel, lax.axis_size("dom")),
        out_shape=jax.ShapeDtypeStruct((1024, 128), BF),
        in_specs=[pl.BlockSpec(memory_space=pl.ANY)] * len(INPUTS),
        out_specs=pl.BlockSpec(memory_space=pltpu.VMEM),
        scratch_shapes=[pltpu.VMEM(shape, dtype) for shape, dtype in held]
        + [
            pltpu.SemaphoreType.DMA((len(INPUTS),)),
            pltpu.SemaphoreType.DMA((8,)),
            pltpu.SemaphoreType.DMA((len(COPIES),)),
            pltpu.SemaphoreType.DMA((len(COPIES),)),
        ],
        compiler_params=pltpu.CompilerParams(
            collective_id=0, has_side_effects=True, vmem_limit_bytes=56 << 20
        ),
    )(*[args[name] for name in INPUTS])


def solution(mesh):
    row = P("dom", None)
    return jax.shard_map(
        local,
        mesh=mesh,
        in_specs=(row,) * 6 + (P("dom"),) + (row,) * 5 + (P(),) * 4,
        out_specs=row,
        check_vma=False,
    )
```

```python
import functools

import jax
import jax.numpy as jnp
from jax import lax
from jax.experimental import pallas as pl
from jax.experimental.pallas import tpu as pltpu
from jax.sharding import PartitionSpec as P

MESH = pl.DeviceIdType.MESH
BF = jnp.bfloat16
F32 = jnp.float32
I32 = jnp.int32


def dot(a, b):
    return jnp.dot(a, b, preferred_element_type=F32)


def dot_nt(a, b):
    return lax.dot_general(a, b, (((1,), (1,)), ((), ())), preferred_element_type=F32)


def onehot(index, rows):
    numbers = lax.broadcasted_iota(jnp.int16, (rows, index.shape[1]), 0)
    return jnp.where(numbers == index.astype(jnp.int16), jnp.ones((), BF), jnp.zeros((), BF))


def half_of(upper, folded):
    return jnp.where(upper == 1, folded[128:], folded[:128])


def centred(weight_t):
    wide = weight_t.astype(F32)
    return (wide - jnp.mean(wide, axis=0, keepdims=True)).astype(BF)


def normalised(values):
    spread = jnp.mean(values * values, axis=0, keepdims=True)
    return values * lax.rsqrt(spread + 1e-05)


def index_row(ref, block):
    rows = ref[block * 8 : block * 8 + 8, :]
    return jnp.concatenate([rows[i : i + 1, :] for i in range(8)], axis=1)


def added(a, b):
    return (a.astype(F32) + b.astype(F32)).astype(BF)


def block_lanes(block):
    return slice(block * 1024, block * 1024 + 1024)


INPUTS = (
    "nodes",
    "edge_in",
    "bound",
    "cluster",
    "fine_send",
    "fine_recv",
    "fine_edges",
    "coarse_bound",
    "edge_out",
    "fine_live",
    "node_in",
    "node_out",
    "coarse_edges",
    "coarse_recv",
    "coarse_send",
    "coarse_live",
)
SCRATCH = dict(
    state=((128, 1024), BF),
    edges_t=((128, 8192), BF),
    before=((128, 8192), F32),
    aggregate=((8, 128, 128), F32),
    recv_table=((8, 128, 128), BF),
    own_table=((256, 512), BF),
    bound_hot=((512, 512), BF),
    cluster_hot=((512, 1024), BF),
    halo_out=((2, 128, 256), BF),
    halo_in=((256, 256), BF),
    later_out=((2, 128, 256), BF),
    later_in=((2, 128, 256), BF),
    w_edge=((3, 3, 128, 128), BF),
    w_message=((3, 128, 128), BF),
    w_node=((3, 128, 256), BF),
    w_update=((3, 128, 128), BF),
    near_out=((2, 8, 256), I32),
    near_in=((2, 8, 256), I32),
    list_in=((1, 128), I32),
    count_out=((16, 512), F32),
    count_in=((3, 16, 512), F32),
    part=((2, 256, 256), BF),
    part_in=((2, 256, 256), BF),
    chip=((2, 256, 256), BF),
    chip_in=((256, 256), BF),
    mine=((2, 128, 256), BF),
    coarse_table=((2, 256, 256), BF),
    rim_out=((4, 64, 128), BF),
    rim_in=((2, 2, 64, 128), BF),
    fresh=((3, 2, 2, 128, 256), BF),
)
COPIES = (
    ["halo_l", "halo_r", "near_l", "near_r", "later_l", "later_r", "list"]
    + ["count1", "count2", "count3", "pool1a", "pool1b", "pool2a", "pool2b", "tablea", "tableb"]
    + ["rim0", "rim1", "rim2", "rim3", "across", "along0", "along1"]
    + ["ahead0", "ahead1", "ahead2", "ahead3", "back0", "back1", "back2", "back3"]
)


class Refs:
    pass


def kernel(total, *refs):
    hbm = dict(zip(INPUTS, refs))
    out_ref = refs[len(INPUTS)]
    r = Refs()
    for name, ref in zip(INPUTS + tuple(SCRATCH), refs[len(INPUTS) + 1 :]):
        setattr(r, name, ref)
    load_sem, edge_sem, send_sem, recv_sem, here_sem = refs[-5:]

    me = lax.axis_index("dom")
    q = lax.rem(me, 4)
    base = me - q
    parity = lax.rem(q, 2)
    half = q // 2
    left = lax.rem(me + total - 1, total)
    right = lax.rem(me + 1, total)
    down = lax.rem(me + total - 4, total)
    up = lax.rem(me + 4, total)
    mate1 = base + q + 1 - 2 * parity
    mate2 = base + q + 2 - 4 * half
    mate3 = base + 3 - q
    mate2_down = lax.rem(mate2 + total - 4, total)
    mate2_up = lax.rem(mate2 + 4, total)
    ahead = lax.rem(base + 4, total)
    back = lax.rem(base + total - 1, total)

    def remote(name, src, dst, device, arrives=None):
        slot = COPIES.index(name)
        return pltpu.make_async_remote_copy(
            src_ref=src,
            dst_ref=dst,
            send_sem=send_sem.at[slot],
            recv_sem=recv_sem.at[slot if arrives is None else arrives],
            device_id=(device,),
            device_id_type=MESH,
        )

    barrier = pltpu.get_barrier_semaphore()

    def greet(device):
        pl.semaphore_signal(barrier, inc=1, device_id=(device,), device_id_type=MESH)

    loads = {}
    for i, name in enumerate(INPUTS):
        if name != "fine_edges":
            loads[name] = pltpu.make_async_copy(hbm[name], getattr(r, name), load_sem.at[i])

    def edge_load(b):
        rows = pl.ds(b * 1024, 1024)
        return pltpu.make_async_copy(
            hbm["fine_edges"].at[rows], r.fine_edges.at[rows], edge_sem.at[b]
        )

    loads["nodes"].start()
    loads["edge_in"].start()
    loads["bound"].start()
    loads["cluster"].start()
    for device in (left, right, mate1, mate2, mate3):
        greet(device)

    for name in INPUTS[4:]:
        if name == "fine_edges":
            for b in range(8):
                edge_load(b).start()
        else:
            loads[name].start()

    def own_part(layer):
        w_edge = r.w_edge[layer, 2]
        for b in range(8):
            send = index_row(r.fine_send, b)
            inside = jnp.where(send < 1024, send & 511, -1)
            gathered = half_of((send >> 9) & 1, dot(r.own_table[...], onehot(inside, 512)))
            hot = onehot(index_row(r.fine_recv, b), 128)
            if layer == 0:
                edge_load(b).wait()
                turned = r.fine_edges[pl.ds(b * 1024, 1024), :].T
                r.edges_t[:, block_lanes(b)] = turned
                joined = jnp.concatenate([r.recv_table[b], w_edge], axis=1)
                rest = dot(joined, jnp.concatenate([hot, turned], axis=0))
            else:
                rest = r.before[:, block_lanes(b)] + dot(r.recv_table[b], hot)
            r.before[:, block_lanes(b)] = gathered + rest

    def fine_rim():
        for b in range(8):
            send = index_row(r.fine_send, b)
            outside = jnp.where(send >= 1024, send & 255, -1)
            r.before[:, block_lanes(b)] += half_of(
                (send >> 8) & 1, dot(r.halo_in[...], onehot(outside, 256))
            )

    def messages(layer, blocks, recv_ref, live_ref, keep):
        w_message = r.w_message[layer]
        for b in blocks:
            lanes = block_lanes(b)
            active = jnp.maximum(r.before[:, lanes], 0.0).astype(BF)
            message = normalised(dot(w_message, active)).astype(BF)
            if keep:
                r.edges_t[:, lanes] = (
                    r.edges_t[:, lanes].astype(F32) + message.astype(F32)
                ).astype(BF)
            target = jnp.where(index_row(live_ref, b) == 1, index_row(recv_ref, b), -1)
            r.aggregate[b] = dot_nt(message, onehot(target, 128))

    def node_update(layer, blocks, own):
        totals = jnp.concatenate([r.aggregate[b] for b in blocks], axis=1)
        joined = jnp.concatenate([own, totals.astype(BF)], axis=0)
        hidden = jnp.maximum(dot(r.w_node[layer], joined), 0.0).astype(BF)
        change = normalised(dot(r.w_update[layer], hidden))
        return (own.astype(F32) + change).astype(BF)

    def fine_tables(layer, own):
        table = dot(r.w_edge[layer, 1], own).astype(BF)
        r.own_table[:128, :] = table[:, :512]
        r.own_table[128:, :] = table[:, 512:]

    def recv_tables(layer, own, blocks):
        table = dot(r.w_edge[layer, 0], own).astype(BF)
        for b in range(blocks):
            r.recv_table[b] = table[:, b * 128 : (b + 1) * 128]

    def lifting(group, side):
        return r.fresh[group, side].reshape(256, 256)

    def lift(group, index):
        hot = onehot(index & 511, 512)
        found = dot(lifting(group, 0), hot[:256]) + dot(lifting(group, 1), hot[256:])
        return half_of(index >> 9, found)

    for name in ("nodes", "edge_in", "bound"):
        loads[name].wait()
    r.state[...] = r.nodes[...].T
    r.w_edge[0, 1] = r.edge_in[0, 1].T
    fine_tables(0, r.state[...])
    rows = r.bound[...]
    r.bound_hot[...] = onehot(rows & 511, 512)
    picked = half_of(rows >> 9, dot(r.own_table[...], r.bound_hot[...])).astype(BF)
    r.halo_out[0] = picked[:, :256]
    r.halo_out[1] = picked[:, 256:]
    halo = (
        remote("halo_l", r.halo_out.at[0], r.halo_in.at[pl.ds(128, 128)], left),
        remote("halo_r", r.halo_out.at[1], r.halo_in.at[pl.ds(0, 128)], right),
    )

    pl.semaphore_wait(barrier, 5)
    for copy in halo:
        copy.start()
    r.w_edge[0, 0] = r.edge_in[0, 0].T
    r.w_edge[0, 2] = r.edge_in[0, 2].T

    loads["cluster"].wait()
    label = index_row(r.cluster, 0)
    digits = []
    for columns in (label[:, :512], label[:, 512:]):
        for digit in (columns & 255, columns >> 8):
            digits.append(jnp.broadcast_to(digit.astype(F32), (8, 512)).astype(BF))
    found = dot(jnp.concatenate(digits, axis=0), r.bound_hot[...])
    upper = jnp.broadcast_to(rows >> 9, (8, 512)) == 1
    low = jnp.where(upper, found[16:24], found[0:8])
    high = jnp.where(upper, found[24:32], found[8:16])
    near = (low + 256.0 * high).astype(I32)
    r.near_out[0] = near[:, :256]
    r.near_out[1] = near[:, 256:]
    r.cluster_hot[...] = onehot(label & 511, 512)
    members = lax.broadcasted_iota(I32, (16, 1024), 0) // 8 == (label >> 9)
    r.count_out[...] = dot_nt(jnp.where(members, 1.0, 0.0).astype(BF), r.cluster_hot[...])
    recv_tables(0, r.state[...], 8)
    loads["coarse_bound"].wait()
    early = (
        remote("near_l", r.near_out.at[0], r.near_in.at[1], left),
        remote("near_r", r.near_out.at[1], r.near_in.at[0], right),
        remote("count1", r.count_out, r.count_in.at[0], mate1),
        remote("count2", r.count_out, r.count_in.at[1], mate2),
        remote("count3", r.count_out, r.count_in.at[2], mate3),
        remote("list", r.coarse_bound, r.list_in, mate2),
    )
    for copy in early:
        copy.start()

    loads["fine_send"].wait()
    loads["fine_recv"].wait()

    own_part(0)
    for name in INPUTS[8:]:
        loads[name].wait()
    for layer in range(3):
        if layer:
            for i in range(3):
                r.w_edge[layer, i] = r.edge_in[layer, i].T
        r.w_message[layer] = centred(r.edge_out[layer].T)
        r.w_node[layer] = r.node_in[layer].T
        r.w_update[layer] = centred(r.node_out[layer].T)
    for copy in halo:
        copy.wait()

    @pl.when((q == 0) | (q == 3))
    def _():
        for device in (mate1, mate2, mate3):
            pl.semaphore_signal(here_sem, inc=1, device_id=(device,), device_id_type=MESH)

    fine_rim()
    messages(0, range(8), r.fine_recv, r.fine_live, True)
    r.state[...] = node_update(0, range(8), r.state[...])

    for copy in early:
        copy.wait()
    share = 1.0 / jnp.maximum(r.count_out[...] + r.count_in[0] + r.count_in[1] + r.count_in[2], 1.0)
    fine = r.state[...]
    nothing = jnp.zeros_like(fine)
    folded = jnp.concatenate(
        [jnp.where(label < 512, fine, nothing), jnp.where(label < 512, nothing, fine)], axis=0
    )
    sums = dot_nt(folded, r.cluster_hot[...])
    for i in range(2):
        means = (sums[i * 128 : i * 128 + 128] * share[i * 8 : i * 8 + 1]).astype(BF)
        for j in range(2):
            r.part[j, i * 128 : i * 128 + 128] = means[:, j * 256 : j * 256 + 256]
    other = 1 - parity
    first = remote("pool1a", r.part.at[other], r.part_in.at[other], mate1)
    second = remote("pool1b", r.part.at[parity], r.part_in.at[parity], mate1)
    first.start()
    second.start()
    first.wait()
    r.chip[parity] = added(r.part[parity], r.part_in[parity])
    pool = []
    for i in range(2):
        rows = pl.ds(i * 128, 128)
        pool.append(remote("pool2" + "ab"[i], r.chip.at[parity, rows], r.chip_in.at[rows], mate2))
        pool[i].start()
    second.wait()
    r.chip[other] = added(r.part[other], r.part_in[other])

    rows = jnp.concatenate([r.coarse_bound[...], r.list_in[...]], axis=1)
    both = jnp.concatenate([r.chip[0], r.chip[1]], axis=1)
    picked = half_of(rows >> 9, dot(both, onehot(rows & 511, 512)))
    r.rim_out[...] = picked.T.astype(BF).reshape(4, 64, 128)
    rims = (
        remote("rim0", r.rim_out.at[0], r.rim_in.at[1, 0], down),
        remote("rim1", r.rim_out.at[1], r.rim_in.at[0, 0], up),
        remote("rim2", r.rim_out.at[2], r.rim_in.at[1, 1], mate2_down),
        remote("rim3", r.rim_out.at[3], r.rim_in.at[0, 1], mate2_up),
    )

    @pl.when((q == 0) | (q == 3))
    def _():
        pl.semaphore_wait(here_sem, 1)

    @pl.when((q == 1) | (q == 2))
    def _():
        pl.semaphore_wait(here_sem, 2)

    for copy in rims:
        copy.start()

    w_send = r.w_edge[1, 1]
    tables = []
    for i in range(2):
        pool[i].wait()
        rows = slice(i * 128, i * 128 + 128)
        r.mine[i] = added(r.chip[parity, rows], r.chip_in[rows])
        r.coarse_table[parity, rows] = dot(w_send, r.mine[i]).astype(BF)
        block = r.coarse_table.at[parity, pl.ds(i * 128, 128)]
        tables.append(remote("table" + "ab"[i], block, block, mate1))
        tables[i].start()
    quarter = r.mine[half]
    recv_tables(1, quarter, 2)

    table = jnp.concatenate([fine[:, :512], fine[:, 512:]], axis=0)
    picked = half_of(r.bound[...] >> 9, dot(table, r.bound_hot[...])).astype(BF)
    r.later_out[0] = picked[:, :256]
    r.later_out[1] = picked[:, 256:]
    later = (
        remote("later_l", r.later_out.at[0], r.later_in.at[1], left),
        remote("later_r", r.later_out.at[1], r.later_in.at[0], right),
    )
    for item in later:
        item.start()

    def coarse_part(b, side):
        send = index_row(r.coarse_send, b)
        inside = jnp.where(((send >> 8) & 1) == side, send & 255, -1)
        hot = onehot(jnp.where(send < 1024, inside, -1), 256)
        return half_of((send >> 9) & 1, dot(r.coarse_table[side], hot))

    w_edge = r.w_edge[1, 2]
    for b in range(2):
        joined = jnp.concatenate([r.recv_table[b], w_edge], axis=1)
        turned = r.coarse_edges[pl.ds(b * 1024, 1024), :].T
        columns = jnp.concatenate([onehot(index_row(r.coarse_recv, b), 128), turned], axis=0)
        r.before[:, block_lanes(b)] = dot(joined, columns) + coarse_part(b, parity)
    for item in tables:
        item.wait()
    for b in range(2):
        r.before[:, block_lanes(b)] += coarse_part(b, other)
    for copy in rims:
        copy.wait()
    rim = (r.rim_in[:, 0].astype(F32) + r.rim_in[:, 1].astype(F32)).astype(BF).reshape(128, 128)
    rim_table = dot_nt(w_send, rim).astype(BF)
    for b in range(2):
        send = index_row(r.coarse_send, b)
        outside = jnp.where(send >= 1024, send & 127, -1)
        r.before[:, block_lanes(b)] += dot(rim_table, onehot(outside, 128))

    messages(1, range(2), r.coarse_recv, r.coarse_live, False)
    r.fresh[1, parity, half] = node_update(1, range(2), quarter)
    own = r.fresh.at[1, parity, half]
    sender = 2 * parity + half
    across = remote("across", own, own, mate2)
    along = remote("along0", own, own, mate1)
    across.start()
    along.start()
    beside = (
        remote("ahead0", own, r.fresh.at[0, parity, half], ahead, COPIES.index("ahead0") + sender),
        remote("back0", own, r.fresh.at[2, parity, half], back, COPIES.index("back0") + sender),
    )
    for item in beside:
        item.start()
    w_edge = r.w_edge[2, 2]
    for b in range(8):
        r.before[:, block_lanes(b)] = dot(w_edge, r.edges_t[:, block_lanes(b)])
    across.wait()
    block = r.fresh.at[1, parity, 1 - half]
    forward = remote("along1", block, block, mate1)
    forward.start()
    found = dot(lifting(1, parity), r.cluster_hot[pl.ds(pl.multiple_of(parity * 256, 256), 256)])
    along.wait()
    forward.wait()
    found += dot(lifting(1, other), r.cluster_hot[pl.ds(pl.multiple_of(other * 256, 256), 256)])
    r.state[...] = (r.state[...].astype(F32) + half_of(label >> 9, found)).astype(BF)

    fine_tables(2, r.state[...])
    recv_tables(2, r.state[...], 8)
    own_part(2)
    for item in later:
        item.wait()
    for item in beside:
        item.wait_send()

    def arrive(name, group):
        for i in range(4):
            block = r.fresh.at[group, i // 2, i % 2]
            remote(name + str(i), block, block, left).wait_recv()

    @pl.when(q == 0)
    def _():
        arrive("ahead", 0)

    @pl.when(q == 3)
    def _():
        arrive("back", 2)

    w_send = r.w_edge[2, 1]
    for side, group in ((0, jnp.where(q == 0, 0, 1)), (1, jnp.where(q == 3, 2, 1))):
        raised = lift(group, r.near_in[side][:1, :])
        rim = (r.later_in[side].astype(F32) + raised).astype(BF)
        r.halo_in[side * 128 : side * 128 + 128] = dot(w_send, rim).astype(BF)
    fine_rim()
    messages(2, range(8), r.fine_recv, r.fine_live, False)
    out_ref[...] = node_update(2, range(8), r.state[...]).T


def local(
    nodes,
    fine_edges,
    fine_recv,
    fine_send,
    fine_live,
    bound_rows,
    cluster,
    coarse_edges,
    coarse_recv,
    coarse_send,
    coarse_live,
    coarse_bound,
    edge_in,
    edge_out,
    node_in,
    node_out,
):
    args = dict(
        nodes=nodes,
        edge_in=edge_in,
        bound=bound_rows,
        cluster=cluster.reshape(8, 128),
        fine_send=fine_send,
        fine_recv=fine_recv,
        fine_edges=fine_edges,
        coarse_bound=coarse_bound,
        edge_out=edge_out,
        fine_live=fine_live,
        node_in=node_in,
        node_out=node_out,
        coarse_edges=coarse_edges,
        coarse_recv=coarse_recv,
        coarse_send=coarse_send,
        coarse_live=coarse_live,
    )
    held = [(args[name].shape, args[name].dtype) for name in INPUTS] + list(SCRATCH.values())
    return pl.pallas_call(
        functools.partial(kernel, lax.axis_size("dom")),
        out_shape=jax.ShapeDtypeStruct((1024, 128), BF),
        in_specs=[pl.BlockSpec(memory_space=pl.ANY)] * len(INPUTS),
        out_specs=pl.BlockSpec(memory_space=pltpu.VMEM),
        scratch_shapes=[pltpu.VMEM(shape, dtype) for shape, dtype in held]
        + [
            pltpu.SemaphoreType.DMA((len(INPUTS),)),
            pltpu.SemaphoreType.DMA((8,)),
            pltpu.SemaphoreType.DMA((len(COPIES),)),
            pltpu.SemaphoreType.DMA((len(COPIES),)),
            pltpu.SemaphoreType.REGULAR,
        ],
        compiler_params=pltpu.CompilerParams(
            collective_id=0, has_side_effects=True, vmem_limit_bytes=56 << 20
        ),
    )(*[args[name] for name in INPUTS])


def solution(mesh):
    row = P("dom", None)
    return jax.shard_map(
        local,
        mesh=mesh,
        in_specs=(row,) * 6 + (P("dom"),) + (row,) * 5 + (P(),) * 4,
        out_specs=row,
        check_vma=False,
    )
```

```python
import functools

import jax
import jax.numpy as jnp
from jax import lax
from jax.experimental import pallas as pl
from jax.experimental.pallas import tpu as pltpu
from jax.sharding import PartitionSpec as P

MESH = pl.DeviceIdType.MESH
BF = jnp.bfloat16
F32 = jnp.float32
I32 = jnp.int32


def dot(a, b):
    return jnp.dot(a, b, preferred_element_type=F32)


def dot_nt(a, b):
    return lax.dot_general(a, b, (((1,), (1,)), ((), ())), preferred_element_type=F32)


def onehot(index, rows):
    numbers = lax.broadcasted_iota(jnp.int16, (rows, index.shape[1]), 0)
    return jnp.where(numbers == index.astype(jnp.int16), jnp.ones((), BF), jnp.zeros((), BF))


def half_of(upper, folded):
    return jnp.where(upper == 1, folded[128:], folded[:128])


def centred(weight_t):
    wide = weight_t.astype(F32)
    return (wide - jnp.mean(wide, axis=0, keepdims=True)).astype(BF)


def normalised(values):
    spread = jnp.mean(values * values, axis=0, keepdims=True)
    return values * lax.rsqrt(spread + 1e-05)


def index_row(ref, block):
    rows = ref[block * 8 : block * 8 + 8, :]
    return jnp.concatenate([rows[i : i + 1, :] for i in range(8)], axis=1)


def added(a, b):
    return (a.astype(F32) + b.astype(F32)).astype(BF)


def block_lanes(block):
    return slice(block * 1024, block * 1024 + 1024)


INPUTS = (
    "nodes",
    "edge_in",
    "bound",
    "cluster",
    "fine_send",
    "fine_recv",
    "fine_edges",
    "coarse_bound",
    "edge_out",
    "fine_live",
    "node_in",
    "node_out",
    "coarse_edges",
    "coarse_recv",
    "coarse_send",
    "coarse_live",
)
SCRATCH = dict(
    state=((128, 1024), BF),
    edges_t=((128, 8192), BF),
    before=((128, 8192), F32),
    aggregate=((8, 128, 128), F32),
    recv_table=((8, 128, 128), BF),
    own_table=((256, 512), BF),
    bound_hot=((512, 512), BF),
    cluster_hot=((512, 1024), BF),
    halo_out=((2, 128, 256), BF),
    halo_in=((256, 256), BF),
    later_out=((2, 128, 256), BF),
    later_in=((2, 128, 256), BF),
    w_edge=((3, 3, 128, 128), BF),
    w_message=((3, 128, 128), BF),
    w_node=((3, 128, 256), BF),
    w_update=((3, 128, 128), BF),
    digits=((32, 512), BF),
    sender_cluster=((8, 1024), F32),
    later_sums=((128, 8192), F32),
    lift_table=((2, 256, 256), BF),
    near_out=((2, 8, 256), I32),
    near_in=((2, 8, 256), I32),
    list_in=((1, 128), I32),
    count_out=((16, 512), F32),
    count_in=((3, 16, 512), F32),
    part=((2, 256, 256), BF),
    part_in=((2, 256, 256), BF),
    chip=((2, 256, 256), BF),
    chip_in=((256, 256), BF),
    mine=((2, 128, 256), BF),
    coarse_table=((2, 256, 256), BF),
    rim_out=((4, 64, 128), BF),
    rim_in=((2, 2, 64, 128), BF),
    fresh=((3, 2, 2, 128, 256), BF),
)
COPIES = (
    ["halo_l", "halo_r", "near_l", "near_r", "later_l", "later_r", "list"]
    + ["count1", "count2", "count3", "pool1a", "pool1b", "pool2a", "pool2b", "tablea", "tableb"]
    + ["rim0", "rim1", "rim2", "rim3", "across", "along0", "along1"]
    + ["ahead0", "ahead1", "ahead2", "ahead3", "back0", "back1", "back2", "back3"]
)


class Refs:
    pass


def kernel(total, *refs):
    hbm = dict(zip(INPUTS, refs))
    out_ref = refs[len(INPUTS)]
    r = Refs()
    for name, ref in zip(INPUTS + tuple(SCRATCH), refs[len(INPUTS) + 1 :]):
        setattr(r, name, ref)
    load_sem, edge_sem, send_sem, recv_sem, here_sem = refs[-5:]

    me = lax.axis_index("dom")
    q = lax.rem(me, 4)
    base = me - q
    parity = lax.rem(q, 2)
    half = q // 2
    left = lax.rem(me + total - 1, total)
    right = lax.rem(me + 1, total)
    down = lax.rem(me + total - 4, total)
    up = lax.rem(me + 4, total)
    mate1 = base + q + 1 - 2 * parity
    mate2 = base + q + 2 - 4 * half
    mate3 = base + 3 - q
    mate2_down = lax.rem(mate2 + total - 4, total)
    mate2_up = lax.rem(mate2 + 4, total)
    ahead = lax.rem(base + 4, total)
    back = lax.rem(base + total - 1, total)

    def remote(name, src, dst, device, arrives=None):
        slot = COPIES.index(name)
        return pltpu.make_async_remote_copy(
            src_ref=src,
            dst_ref=dst,
            send_sem=send_sem.at[slot],
            recv_sem=recv_sem.at[slot if arrives is None else arrives],
            device_id=(device,),
            device_id_type=MESH,
        )

    barrier = pltpu.get_barrier_semaphore()

    def greet(device):
        pl.semaphore_signal(barrier, inc=1, device_id=(device,), device_id_type=MESH)

    loads = {}
    for i, name in enumerate(INPUTS):
        if name not in ("fine_edges", "edge_in"):
            loads[name] = pltpu.make_async_copy(hbm[name], getattr(r, name), load_sem.at[i])

    def edge_load(b):
        rows = pl.ds(b * 1024, 1024)
        return pltpu.make_async_copy(
            hbm["fine_edges"].at[rows], r.fine_edges.at[rows], edge_sem.at[b]
        )

    first_weights = pltpu.make_async_copy(
        hbm["edge_in"].at[0], r.edge_in.at[0], load_sem.at[len(INPUTS)]
    )
    loads["edge_in"] = pltpu.make_async_copy(
        hbm["edge_in"].at[pl.ds(1, 2)], r.edge_in.at[pl.ds(1, 2)], load_sem.at[1]
    )
    loads["nodes"].start()
    first_weights.start()
    loads["bound"].start()
    loads["cluster"].start()
    for device in (left, right, mate1, mate2, mate3):
        greet(device)

    def first_sums():
        w_edge = r.w_edge[0, 2]
        for b in range(8):
            send = index_row(r.fine_send, b)
            inside = jnp.where(send < 1024, send & 511, -1)
            gathered = half_of((send >> 9) & 1, dot(r.own_table[...], onehot(inside, 512)))
            edge_load(b).wait()
            turned = r.fine_edges[pl.ds(b * 1024, 1024), :].T
            r.edges_t[:, block_lanes(b)] = turned
            joined = jnp.concatenate([r.recv_table[b], w_edge], axis=1)
            columns = jnp.concatenate([onehot(index_row(r.fine_recv, b), 128), turned], axis=0)
            r.before[:, block_lanes(b)] = gathered + dot(joined, columns)

    def digits_of(upper, found):
        low = jnp.where(upper == 1, found[16:17], found[0:1])
        high = jnp.where(upper == 1, found[24:25], found[8:9])
        return low + 256.0 * high

    def later_own(blocks):
        table = jnp.concatenate([r.own_table[...], r.digits[...]], axis=0)
        for b in blocks:
            send = index_row(r.fine_send, b)
            upper = (send >> 9) & 1
            found = dot(table, onehot(jnp.where(send < 1024, send & 511, -1), 512))
            r.sender_cluster[b : b + 1, :] = digits_of(upper, found[256:])
            r.later_sums[:, block_lanes(b)] = half_of(upper, found[:256]) + dot(
                r.w_edge[2, 2], r.edges_t[:, block_lanes(b)]
            )

    def later_rim():
        near = r.near_in[...]
        digits = []
        for i in range(2):
            for digit in (near[i] & 255, near[i] >> 8):
                digits.append(digit.astype(F32).astype(BF))
        table = jnp.concatenate([r.halo_in[...]] + digits, axis=0)
        for b in range(8):
            send = index_row(r.fine_send, b)
            upper = (send >> 8) & 1
            found = dot(table, onehot(jnp.where(send >= 1024, send & 255, -1), 256))
            r.sender_cluster[b : b + 1, :] += digits_of(upper, found[256:])
            r.later_sums[:, block_lanes(b)] += half_of(upper, found[:256])

    def lifted_sums():
        table = jnp.concatenate([r.lift_table[0], r.lift_table[1]], axis=1)
        for b in range(8):
            place = index_row(r.fine_send, b) >> 8
            cluster = r.sender_cluster[b : b + 1, :].astype(I32)
            beside = ((place == 4) & (q == 0)) | ((place == 5) & (q == 3))
            found = dot(table, onehot(jnp.where(beside, -1, cluster & 511), 512))
            r.before[:, block_lanes(b)] = (
                r.later_sums[:, block_lanes(b)]
                + half_of(cluster >> 9, found)
                + dot(r.recv_table[b], onehot(index_row(r.fine_recv, b), 128))
            )

    def fine_rim():
        for b in range(8):
            send = index_row(r.fine_send, b)
            outside = jnp.where(send >= 1024, send & 255, -1)
            r.before[:, block_lanes(b)] += half_of(
                (send >> 8) & 1, dot(r.halo_in[...], onehot(outside, 256))
            )

    def messages(layer, blocks, recv_ref, live_ref, keep):
        w_message = r.w_message[layer]
        for b in blocks:
            lanes = block_lanes(b)
            active = jnp.maximum(r.before[:, lanes], 0.0).astype(BF)
            message = normalised(dot(w_message, active)).astype(BF)
            if keep:
                r.edges_t[:, lanes] = (
                    r.edges_t[:, lanes].astype(F32) + message.astype(F32)
                ).astype(BF)
            target = jnp.where(index_row(live_ref, b) == 1, index_row(recv_ref, b), -1)
            r.aggregate[b] = dot_nt(message, onehot(target, 128))

    def node_update(layer, blocks, own):
        totals = jnp.concatenate([r.aggregate[b] for b in blocks], axis=1)
        joined = jnp.concatenate([own, totals.astype(BF)], axis=0)
        hidden = jnp.maximum(dot(r.w_node[layer], joined), 0.0).astype(BF)
        change = normalised(dot(r.w_update[layer], hidden))
        return (own.astype(F32) + change).astype(BF)

    def fine_tables(layer, own):
        table = dot(r.w_edge[layer, 1], own).astype(BF)
        r.own_table[:128, :] = table[:, :512]
        r.own_table[128:, :] = table[:, 512:]

    def recv_tables(layer, own, blocks):
        table = dot(r.w_edge[layer, 0], own).astype(BF)
        for b in range(blocks):
            r.recv_table[b] = table[:, b * 128 : (b + 1) * 128]

    def lifting(group, side):
        return r.fresh[group, side].reshape(256, 256)

    def raise_table(side):
        for i in range(2):
            rows = slice(i * 128, i * 128 + 128)
            r.lift_table[side, rows] = dot(r.w_edge[2, 1], r.fresh[1, side, i]).astype(BF)

    def lift(group, index):
        hot = onehot(index & 511, 512)
        found = dot(lifting(group, 0), hot[:256]) + dot(lifting(group, 1), hot[256:])
        return half_of(index >> 9, found)

    loads["nodes"].wait()
    first_weights.wait()
    loads["bound"].wait()
    for name in INPUTS[4:] + ("edge_in",):
        if name == "fine_edges":
            for b in range(8):
                edge_load(b).start()
        else:
            loads[name].start()
    r.state[...] = r.nodes[...].T
    r.w_edge[0, 1] = r.edge_in[0, 1].T
    fine_tables(0, r.state[...])
    rows = r.bound[...]
    r.bound_hot[...] = onehot(rows & 511, 512)
    picked = half_of(rows >> 9, dot(r.own_table[...], r.bound_hot[...])).astype(BF)
    r.halo_out[0] = picked[:, :256]
    r.halo_out[1] = picked[:, 256:]
    halo = (
        remote("halo_l", r.halo_out.at[0], r.halo_in.at[pl.ds(128, 128)], left),
        remote("halo_r", r.halo_out.at[1], r.halo_in.at[pl.ds(0, 128)], right),
    )

    pl.semaphore_wait(barrier, 5)
    for copy in halo:
        copy.start()
    r.w_edge[0, 0] = r.edge_in[0, 0].T
    r.w_edge[0, 2] = r.edge_in[0, 2].T

    loads["cluster"].wait()
    label = index_row(r.cluster, 0)
    digits = []
    for columns in (label[:, :512], label[:, 512:]):
        for digit in (columns & 255, columns >> 8):
            digits.append(jnp.broadcast_to(digit.astype(F32), (8, 512)).astype(BF))
    r.digits[...] = jnp.concatenate(digits, axis=0)
    found = dot(r.digits[...], r.bound_hot[...])
    upper = jnp.broadcast_to(rows >> 9, (8, 512)) == 1
    low = jnp.where(upper, found[16:24], found[0:8])
    high = jnp.where(upper, found[24:32], found[8:16])
    near = (low + 256.0 * high).astype(I32)
    r.near_out[0] = near[:, :256]
    r.near_out[1] = near[:, 256:]
    r.cluster_hot[...] = onehot(label & 511, 512)
    members = lax.broadcasted_iota(I32, (16, 1024), 0) // 8 == (label >> 9)
    r.count_out[...] = dot_nt(jnp.where(members, 1.0, 0.0).astype(BF), r.cluster_hot[...])
    recv_tables(0, r.state[...], 8)
    loads["coarse_bound"].wait()
    early = (
        remote("near_l", r.near_out.at[0], r.near_in.at[1], left),
        remote("near_r", r.near_out.at[1], r.near_in.at[0], right),
        remote("count1", r.count_out, r.count_in.at[0], mate1),
        remote("count2", r.count_out, r.count_in.at[1], mate2),
        remote("count3", r.count_out, r.count_in.at[2], mate3),
        remote("list", r.coarse_bound, r.list_in, mate2),
    )
    for copy in early:
        copy.start()

    loads["fine_send"].wait()
    loads["fine_recv"].wait()

    first_sums()
    for name in INPUTS[8:] + ("edge_in",):
        loads[name].wait()
    for layer in range(3):
        if layer:
            for i in range(3):
                r.w_edge[layer, i] = r.edge_in[layer, i].T
        r.w_message[layer] = centred(r.edge_out[layer].T)
        r.w_node[layer] = r.node_in[layer].T
        r.w_update[layer] = centred(r.node_out[layer].T)
    for copy in halo:
        copy.wait()

    @pl.when((q == 0) | (q == 3))
    def _():
        for device in (mate1, mate2, mate3):
            pl.semaphore_signal(here_sem, inc=1, device_id=(device,), device_id_type=MESH)

    fine_rim()
    messages(0, range(8), r.fine_recv, r.fine_live, True)
    r.state[...] = node_update(0, range(8), r.state[...])

    for copy in early:
        copy.wait()
    share = 1.0 / jnp.maximum(r.count_out[...] + r.count_in[0] + r.count_in[1] + r.count_in[2], 1.0)
    fine = r.state[...]
    nothing = jnp.zeros_like(fine)
    folded = jnp.concatenate(
        [jnp.where(label < 512, fine, nothing), jnp.where(label < 512, nothing, fine)], axis=0
    )
    sums = dot_nt(folded, r.cluster_hot[...])
    for i in range(2):
        means = (sums[i * 128 : i * 128 + 128] * share[i * 8 : i * 8 + 1]).astype(BF)
        for j in range(2):
            r.part[j, i * 128 : i * 128 + 128] = means[:, j * 256 : j * 256 + 256]
    other = 1 - parity
    first = remote("pool1a", r.part.at[other], r.part_in.at[other], mate1)
    second = remote("pool1b", r.part.at[parity], r.part_in.at[parity], mate1)
    first.start()
    second.start()
    first.wait()
    r.chip[parity] = added(r.part[parity], r.part_in[parity])
    pool = []
    for i in range(2):
        rows = pl.ds(i * 128, 128)
        pool.append(remote("pool2" + "ab"[i], r.chip.at[parity, rows], r.chip_in.at[rows], mate2))
        pool[i].start()
    second.wait()
    r.chip[other] = added(r.part[other], r.part_in[other])

    rows = jnp.concatenate([r.coarse_bound[...], r.list_in[...]], axis=1)
    both = jnp.concatenate([r.chip[0], r.chip[1]], axis=1)
    picked = half_of(rows >> 9, dot(both, onehot(rows & 511, 512)))
    r.rim_out[...] = picked.T.astype(BF).reshape(4, 64, 128)
    rims = (
        remote("rim0", r.rim_out.at[0], r.rim_in.at[1, 0], down),
        remote("rim1", r.rim_out.at[1], r.rim_in.at[0, 0], up),
        remote("rim2", r.rim_out.at[2], r.rim_in.at[1, 1], mate2_down),
        remote("rim3", r.rim_out.at[3], r.rim_in.at[0, 1], mate2_up),
    )

    @pl.when((q == 0) | (q == 3))
    def _():
        pl.semaphore_wait(here_sem, 1)

    @pl.when((q == 1) | (q == 2))
    def _():
        pl.semaphore_wait(here_sem, 2)

    for copy in rims:
        copy.start()

    table = jnp.concatenate([fine[:, :512], fine[:, 512:]], axis=0)
    picked = half_of(r.bound[...] >> 9, dot(table, r.bound_hot[...])).astype(BF)
    r.later_out[0] = picked[:, :256]
    r.later_out[1] = picked[:, 256:]
    later = (
        remote("later_l", r.later_out.at[0], r.later_in.at[1], left),
        remote("later_r", r.later_out.at[1], r.later_in.at[0], right),
    )
    for item in later:
        item.start()
    fine_tables(2, fine)
    later_own(range(4))

    w_send = r.w_edge[1, 1]
    tables = []
    for i in range(2):
        pool[i].wait()
        rows = slice(i * 128, i * 128 + 128)
        r.mine[i] = added(r.chip[parity, rows], r.chip_in[rows])
        r.coarse_table[parity, rows] = dot(w_send, r.mine[i]).astype(BF)
        block = r.coarse_table.at[parity, pl.ds(i * 128, 128)]
        tables.append(remote("table" + "ab"[i], block, block, mate1))
        tables[i].start()
    quarter = r.mine[half]
    recv_tables(1, quarter, 2)

    def coarse_part(b, side):
        send = index_row(r.coarse_send, b)
        inside = jnp.where(((send >> 8) & 1) == side, send & 255, -1)
        hot = onehot(jnp.where(send < 1024, inside, -1), 256)
        return half_of((send >> 9) & 1, dot(r.coarse_table[side], hot))

    w_edge = r.w_edge[1, 2]
    for b in range(2):
        joined = jnp.concatenate([r.recv_table[b], w_edge], axis=1)
        turned = r.coarse_edges[pl.ds(b * 1024, 1024), :].T
        columns = jnp.concatenate([onehot(index_row(r.coarse_recv, b), 128), turned], axis=0)
        r.before[:, block_lanes(b)] = dot(joined, columns) + coarse_part(b, parity)
    for item in tables:
        item.wait()
    for b in range(2):
        r.before[:, block_lanes(b)] += coarse_part(b, other)
    for copy in rims:
        copy.wait()
    rim = (r.rim_in[:, 0].astype(F32) + r.rim_in[:, 1].astype(F32)).astype(BF).reshape(128, 128)
    rim_table = dot_nt(w_send, rim).astype(BF)
    for b in range(2):
        send = index_row(r.coarse_send, b)
        outside = jnp.where(send >= 1024, send & 127, -1)
        r.before[:, block_lanes(b)] += dot(rim_table, onehot(outside, 128))

    messages(1, range(2), r.coarse_recv, r.coarse_live, False)
    r.fresh[1, parity, half] = node_update(1, range(2), quarter)
    own = r.fresh.at[1, parity, half]
    sender = 2 * parity + half
    across = remote("across", own, own, mate2)
    along = remote("along0", own, own, mate1)
    across.start()
    along.start()
    beside = (
        remote("ahead0", own, r.fresh.at[0, parity, half], ahead, COPIES.index("ahead0") + sender),
        remote("back0", own, r.fresh.at[2, parity, half], back, COPIES.index("back0") + sender),
    )
    for item in beside:
        item.start()
    later_own(range(4, 8))
    for item in later:
        item.wait()
    for i in range(2):
        r.halo_in[i * 128 : i * 128 + 128] = dot(r.w_edge[2, 1], r.later_in[i]).astype(BF)
    later_rim()
    across.wait()
    block = r.fresh.at[1, parity, 1 - half]
    forward = remote("along1", block, block, mate1)
    forward.start()
    raise_table(parity)
    found = dot(lifting(1, parity), r.cluster_hot[pl.ds(pl.multiple_of(parity * 256, 256), 256)])
    along.wait()
    forward.wait()
    raise_table(other)
    found += dot(lifting(1, other), r.cluster_hot[pl.ds(pl.multiple_of(other * 256, 256), 256)])
    r.state[...] = (r.state[...].astype(F32) + half_of(label >> 9, found)).astype(BF)

    recv_tables(2, r.state[...], 8)
    lifted_sums()
    for item in beside:
        item.wait_send()

    def arrive(name, group):
        for i in range(4):
            block = r.fresh.at[group, i // 2, i % 2]
            remote(name + str(i), block, block, left).wait_recv()

    @pl.when(q == 0)
    def _():
        arrive("ahead", 0)

    @pl.when(q == 3)
    def _():
        arrive("back", 2)

    @pl.when((q == 0) | (q == 3))
    def _():
        side = jnp.where(q == 0, 0, 1)
        raised = lift(2 * side, r.near_in[side][:1, :]).astype(BF)
        table = dot(r.w_edge[2, 1], raised).astype(BF)
        for b in range(8):
            send = index_row(r.fine_send, b)
            outside = jnp.where((send >> 8) == 4 + side, send & 255, -1)
            r.before[:, block_lanes(b)] += dot(table, onehot(outside, 256))

    messages(2, range(8), r.fine_recv, r.fine_live, False)
    out_ref[...] = node_update(2, range(8), r.state[...]).T


def local(
    nodes,
    fine_edges,
    fine_recv,
    fine_send,
    fine_live,
    bound_rows,
    cluster,
    coarse_edges,
    coarse_recv,
    coarse_send,
    coarse_live,
    coarse_bound,
    edge_in,
    edge_out,
    node_in,
    node_out,
):
    args = dict(
        nodes=nodes,
        edge_in=edge_in,
        bound=bound_rows,
        cluster=cluster.reshape(8, 128),
        fine_send=fine_send,
        fine_recv=fine_recv,
        fine_edges=fine_edges,
        coarse_bound=coarse_bound,
        edge_out=edge_out,
        fine_live=fine_live,
        node_in=node_in,
        node_out=node_out,
        coarse_edges=coarse_edges,
        coarse_recv=coarse_recv,
        coarse_send=coarse_send,
        coarse_live=coarse_live,
    )
    held = [(args[name].shape, args[name].dtype) for name in INPUTS] + list(SCRATCH.values())
    return pl.pallas_call(
        functools.partial(kernel, lax.axis_size("dom")),
        out_shape=jax.ShapeDtypeStruct((1024, 128), BF),
        in_specs=[pl.BlockSpec(memory_space=pl.ANY)] * len(INPUTS),
        out_specs=pl.BlockSpec(memory_space=pltpu.VMEM),
        scratch_shapes=[pltpu.VMEM(shape, dtype) for shape, dtype in held]
        + [
            pltpu.SemaphoreType.DMA((len(INPUTS) + 1,)),
            pltpu.SemaphoreType.DMA((8,)),
            pltpu.SemaphoreType.DMA((len(COPIES),)),
            pltpu.SemaphoreType.DMA((len(COPIES),)),
            pltpu.SemaphoreType.REGULAR,
        ],
        compiler_params=pltpu.CompilerParams(
            collective_id=0, has_side_effects=True, vmem_limit_bytes=56 << 20
        ),
    )(*[args[name] for name in INPUTS])


def solution(mesh):
    row = P("dom", None)
    return jax.shard_map(
        local,
        mesh=mesh,
        in_specs=(row,) * 6 + (P("dom"),) + (row,) * 5 + (P(),) * 4,
        out_specs=row,
        check_vma=False,
    )
```

```python
import functools

import jax
import jax.numpy as jnp
from jax import lax
from jax.experimental import pallas as pl
from jax.experimental.pallas import tpu as pltpu
from jax.sharding import PartitionSpec as P

MESH = pl.DeviceIdType.MESH
BF = jnp.bfloat16
F32 = jnp.float32
I32 = jnp.int32


def dot(a, b):
    return jnp.dot(a, b, preferred_element_type=F32)


def dot_nt(a, b):
    return lax.dot_general(a, b, (((1,), (1,)), ((), ())), preferred_element_type=F32)


def onehot(index, rows):
    numbers = lax.broadcasted_iota(jnp.int16, (rows, index.shape[1]), 0)
    return jnp.where(numbers == index.astype(jnp.int16), jnp.ones((), BF), jnp.zeros((), BF))


def half_of(upper, folded):
    return jnp.where(upper == 1, folded[128:], folded[:128])


def centred(weight_t):
    wide = weight_t.astype(F32)
    return (wide - jnp.mean(wide, axis=0, keepdims=True)).astype(BF)


def normalised(values):
    spread = jnp.mean(values * values, axis=0, keepdims=True)
    return values * lax.rsqrt(spread + 1e-05)


def index_row(ref, block):
    rows = ref[block * 8 : block * 8 + 8, :]
    return jnp.concatenate([rows[i : i + 1, :] for i in range(8)], axis=1)


def added(a, b):
    return (a.astype(F32) + b.astype(F32)).astype(BF)


def block_lanes(block):
    return slice(block * 1024, block * 1024 + 1024)


INPUTS = (
    "nodes",
    "edge_in",
    "bound",
    "cluster",
    "fine_send",
    "fine_recv",
    "fine_edges",
    "coarse_bound",
    "edge_out",
    "fine_live",
    "node_in",
    "node_out",
    "coarse_edges",
    "coarse_recv",
    "coarse_send",
    "coarse_live",
)
SCRATCH = dict(
    state=((128, 1024), BF),
    edges_t=((128, 8192), BF),
    before=((128, 8192), F32),
    aggregate=((8, 128, 128), F32),
    recv_table=((8, 128, 128), BF),
    own_table=((256, 512), BF),
    bound_hot=((512, 512), BF),
    cluster_hot=((512, 1024), BF),
    halo_out=((2, 128, 256), BF),
    halo_in=((256, 256), BF),
    later_out=((2, 128, 256), BF),
    later_in=((2, 128, 256), BF),
    w_edge=((3, 3, 128, 128), BF),
    w_message=((3, 128, 128), BF),
    w_node=((3, 128, 256), BF),
    w_update=((3, 128, 128), BF),
    digits=((32, 512), BF),
    sender_cluster=((8, 1024), F32),
    later_sums=((128, 8192), F32),
    lift_table=((2, 256, 256), BF),
    near_out=((2, 8, 256), I32),
    near_in=((2, 8, 256), I32),
    list_in=((1, 128), I32),
    count_out=((16, 512), F32),
    count_in=((3, 16, 512), F32),
    part=((2, 256, 256), BF),
    part_in=((2, 256, 256), BF),
    chip=((2, 256, 256), BF),
    chip_in=((256, 256), BF),
    mine=((2, 128, 256), BF),
    coarse_table=((2, 256, 256), BF),
    rim_out=((4, 64, 128), BF),
    rim_in=((2, 2, 64, 128), BF),
    fresh=((3, 2, 2, 128, 256), BF),
)
COPIES = (
    ["halo_l", "halo_r", "near_l", "near_r", "later_l", "later_r", "list"]
    + ["count1", "count2", "count3", "pool1a", "pool1b", "pool2a", "pool2b", "tablea", "tableb"]
    + ["rim0", "rim1", "rim2", "rim3", "across", "along0", "along1"]
    + ["ahead0", "ahead1", "ahead2", "ahead3", "back0", "back1", "back2", "back3"]
)


class Refs:
    pass


def kernel(total, *refs):
    hbm = dict(zip(INPUTS, refs))
    out_ref = refs[len(INPUTS)]
    r = Refs()
    for name, ref in zip(INPUTS + tuple(SCRATCH), refs[len(INPUTS) + 1 :]):
        setattr(r, name, ref)
    load_sem, edge_sem, send_sem, recv_sem, here_sem = refs[-5:]

    me = lax.axis_index("dom")
    q = lax.rem(me, 4)
    base = me - q
    parity = lax.rem(q, 2)
    half = q // 2
    left = lax.rem(me + total - 1, total)
    right = lax.rem(me + 1, total)
    down = lax.rem(me + total - 4, total)
    up = lax.rem(me + 4, total)
    mate1 = base + q + 1 - 2 * parity
    mate2 = base + q + 2 - 4 * half
    mate3 = base + 3 - q
    mate2_down = lax.rem(mate2 + total - 4, total)
    mate2_up = lax.rem(mate2 + 4, total)
    ahead = lax.rem(base + 4, total)
    back = lax.rem(base + total - 1, total)

    def remote(name, src, dst, device, arrives=None):
        slot = COPIES.index(name)
        return pltpu.make_async_remote_copy(
            src_ref=src,
            dst_ref=dst,
            send_sem=send_sem.at[slot],
            recv_sem=recv_sem.at[slot if arrives is None else arrives],
            device_id=(device,),
            device_id_type=MESH,
        )

    barrier = pltpu.get_barrier_semaphore()

    def greet(device):
        pl.semaphore_signal(barrier, inc=1, device_id=(device,), device_id_type=MESH)

    loads = {}
    for i, name in enumerate(INPUTS):
        if name not in ("fine_edges", "edge_in"):
            loads[name] = pltpu.make_async_copy(hbm[name], getattr(r, name), load_sem.at[i])

    def edge_load(b):
        rows = pl.ds(b * 1024, 1024)
        return pltpu.make_async_copy(
            hbm["fine_edges"].at[rows], r.fine_edges.at[rows], edge_sem.at[b]
        )

    first_weights = pltpu.make_async_copy(
        hbm["edge_in"].at[0], r.edge_in.at[0], load_sem.at[len(INPUTS)]
    )
    loads["edge_in"] = pltpu.make_async_copy(
        hbm["edge_in"].at[pl.ds(1, 2)], r.edge_in.at[pl.ds(1, 2)], load_sem.at[1]
    )
    loads["nodes"].start()
    first_weights.start()
    loads["bound"].start()
    loads["cluster"].start()
    for device in (left, right, mate1, mate2, mate3):
        greet(device)

    def first_sums():
        w_edge = r.w_edge[0, 2]
        for b in range(8):
            send = index_row(r.fine_send, b)
            inside = jnp.where(send < 1024, send & 511, -1)
            gathered = half_of((send >> 9) & 1, dot(r.own_table[...], onehot(inside, 512)))
            edge_load(b).wait()
            turned = r.fine_edges[pl.ds(b * 1024, 1024), :].T
            r.edges_t[:, block_lanes(b)] = turned
            joined = jnp.concatenate([r.recv_table[b], w_edge], axis=1)
            columns = jnp.concatenate([onehot(index_row(r.fine_recv, b), 128), turned], axis=0)
            r.before[:, block_lanes(b)] = gathered + dot(joined, columns)

    def digits_of(upper, found):
        low = jnp.where(upper == 1, found[16:17], found[0:1])
        high = jnp.where(upper == 1, found[24:25], found[8:9])
        return low + 256.0 * high

    def later_own(blocks):
        table = jnp.concatenate([r.own_table[...], r.digits[...]], axis=0)
        for b in blocks:
            send = index_row(r.fine_send, b)
            upper = (send >> 9) & 1
            found = dot(table, onehot(jnp.where(send < 1024, send & 511, -1), 512))
            r.sender_cluster[b : b + 1, :] = digits_of(upper, found[256:])
            r.later_sums[:, block_lanes(b)] = half_of(upper, found[:256]) + dot(
                r.w_edge[2, 2], r.edges_t[:, block_lanes(b)]
            )

    def later_rim():
        near = r.near_in[...]
        digits = []
        for i in range(2):
            for digit in (near[i] & 255, near[i] >> 8):
                digits.append(digit.astype(F32).astype(BF))
        table = jnp.concatenate([r.halo_in[...]] + digits, axis=0)
        for b in range(8):
            send = index_row(r.fine_send, b)
            upper = (send >> 8) & 1
            found = dot(table, onehot(jnp.where(send >= 1024, send & 255, -1), 256))
            r.sender_cluster[b : b + 1, :] += digits_of(upper, found[256:])
            r.later_sums[:, block_lanes(b)] += half_of(upper, found[:256])

    def lifted_sums():
        table = jnp.concatenate([r.lift_table[0], r.lift_table[1]], axis=1)
        for b in range(8):
            place = index_row(r.fine_send, b) >> 8
            cluster = r.sender_cluster[b : b + 1, :].astype(I32)
            beside = ((place == 4) & (q == 0)) | ((place == 5) & (q == 3))
            found = dot(table, onehot(jnp.where(beside, -1, cluster & 511), 512))
            r.before[:, block_lanes(b)] = (
                r.later_sums[:, block_lanes(b)]
                + half_of(cluster >> 9, found)
                + dot(r.recv_table[b], onehot(index_row(r.fine_recv, b), 128))
            )

    def fine_rim():
        for b in range(8):
            send = index_row(r.fine_send, b)
            outside = jnp.where(send >= 1024, send & 255, -1)
            r.before[:, block_lanes(b)] += half_of(
                (send >> 8) & 1, dot(r.halo_in[...], onehot(outside, 256))
            )

    def messages(layer, blocks, recv_ref, live_ref, keep):
        w_message = r.w_message[layer]
        for b in blocks:
            lanes = block_lanes(b)
            active = jnp.maximum(r.before[:, lanes], 0.0).astype(BF)
            message = normalised(dot(w_message, active)).astype(BF)
            if keep:
                r.edges_t[:, lanes] = (
                    r.edges_t[:, lanes].astype(F32) + message.astype(F32)
                ).astype(BF)
            target = jnp.where(index_row(live_ref, b) == 1, index_row(recv_ref, b), -1)
            r.aggregate[b] = dot_nt(message, onehot(target, 128))

    def node_update(layer, blocks, own):
        totals = jnp.concatenate([r.aggregate[b] for b in blocks], axis=1)
        joined = jnp.concatenate([own, totals.astype(BF)], axis=0)
        hidden = jnp.maximum(dot(r.w_node[layer], joined), 0.0).astype(BF)
        change = normalised(dot(r.w_update[layer], hidden))
        return (own.astype(F32) + change).astype(BF)

    def fine_tables(layer, own):
        table = dot(r.w_edge[layer, 1], own).astype(BF)
        r.own_table[:128, :] = table[:, :512]
        r.own_table[128:, :] = table[:, 512:]

    def recv_tables(layer, own, blocks):
        table = dot(r.w_edge[layer, 0], own).astype(BF)
        for b in range(blocks):
            r.recv_table[b] = table[:, b * 128 : (b + 1) * 128]

    def lifting(group, side):
        return r.fresh[group, side].reshape(256, 256)

    def raise_table(side):
        for i in range(2):
            rows = slice(i * 128, i * 128 + 128)
            r.lift_table[side, rows] = dot(r.w_edge[2, 1], r.fresh[1, side, i]).astype(BF)

    def lift(group, index):
        hot = onehot(index & 511, 512)
        found = dot(lifting(group, 0), hot[:256]) + dot(lifting(group, 1), hot[256:])
        return half_of(index >> 9, found)

    loads["nodes"].wait()
    first_weights.wait()
    loads["bound"].wait()
    for name in INPUTS[4:] + ("edge_in",):
        if name == "fine_edges":
            for b in range(8):
                edge_load(b).start()
        else:
            loads[name].start()
    r.state[...] = r.nodes[...].T
    r.w_edge[0, 1] = r.edge_in[0, 1].T
    fine_tables(0, r.state[...])
    rows = r.bound[...]
    r.bound_hot[...] = onehot(rows & 511, 512)
    picked = half_of(rows >> 9, dot(r.own_table[...], r.bound_hot[...])).astype(BF)
    r.halo_out[0] = picked[:, :256]
    r.halo_out[1] = picked[:, 256:]
    halo = (
        remote("halo_l", r.halo_out.at[0], r.halo_in.at[pl.ds(128, 128)], left),
        remote("halo_r", r.halo_out.at[1], r.halo_in.at[pl.ds(0, 128)], right),
    )

    pl.semaphore_wait(barrier, 5)
    for copy in halo:
        copy.start()
    r.w_edge[0, 0] = r.edge_in[0, 0].T
    r.w_edge[0, 2] = r.edge_in[0, 2].T

    loads["cluster"].wait()
    label = index_row(r.cluster, 0)
    digits = []
    for columns in (label[:, :512], label[:, 512:]):
        for digit in (columns & 255, columns >> 8):
            digits.append(jnp.broadcast_to(digit.astype(F32), (8, 512)).astype(BF))
    r.digits[...] = jnp.concatenate(digits, axis=0)
    found = dot(r.digits[...], r.bound_hot[...])
    upper = jnp.broadcast_to(rows >> 9, (8, 512)) == 1
    low = jnp.where(upper, found[16:24], found[0:8])
    high = jnp.where(upper, found[24:32], found[8:16])
    near = (low + 256.0 * high).astype(I32)
    r.near_out[0] = near[:, :256]
    r.near_out[1] = near[:, 256:]
    r.cluster_hot[...] = onehot(label & 511, 512)
    members = lax.broadcasted_iota(I32, (16, 1024), 0) // 8 == (label >> 9)
    r.count_out[...] = dot_nt(jnp.where(members, 1.0, 0.0).astype(BF), r.cluster_hot[...])
    recv_tables(0, r.state[...], 8)
    loads["coarse_bound"].wait()
    early = (
        remote("near_l", r.near_out.at[0], r.near_in.at[1], left),
        remote("near_r", r.near_out.at[1], r.near_in.at[0], right),
        remote("count1", r.count_out, r.count_in.at[0], mate1),
        remote("count2", r.count_out, r.count_in.at[1], mate2),
        remote("count3", r.count_out, r.count_in.at[2], mate3),
        remote("list", r.coarse_bound, r.list_in, mate2),
    )
    for copy in early:
        copy.start()

    loads["fine_send"].wait()
    loads["fine_recv"].wait()

    first_sums()
    for name in INPUTS[8:] + ("edge_in",):
        loads[name].wait()
    for layer in range(3):
        if layer:
            for i in range(3):
                r.w_edge[layer, i] = r.edge_in[layer, i].T
        r.w_message[layer] = centred(r.edge_out[layer].T)
        r.w_node[layer] = r.node_in[layer].T
        r.w_update[layer] = centred(r.node_out[layer].T)
    for copy in halo:
        copy.wait()

    @pl.when((q == 0) | (q == 3))
    def _():
        for device in (mate1, mate2, mate3):
            pl.semaphore_signal(here_sem, inc=1, device_id=(device,), device_id_type=MESH)

    fine_rim()
    messages(0, range(8), r.fine_recv, r.fine_live, True)
    r.state[...] = node_update(0, range(8), r.state[...])

    for copy in early:
        copy.wait()
    share = 1.0 / jnp.maximum(r.count_out[...] + r.count_in[0] + r.count_in[1] + r.count_in[2], 1.0)
    fine = r.state[...]
    nothing = jnp.zeros_like(fine)
    folded = jnp.concatenate(
        [jnp.where(label < 512, fine, nothing), jnp.where(label < 512, nothing, fine)], axis=0
    )
    sums = dot_nt(folded, r.cluster_hot[...])
    for i in range(2):
        means = (sums[i * 128 : i * 128 + 128] * share[i * 8 : i * 8 + 1]).astype(BF)
        for j in range(2):
            r.part[j, i * 128 : i * 128 + 128] = means[:, j * 256 : j * 256 + 256]
    other = 1 - parity
    first = remote("pool1a", r.part.at[other], r.part_in.at[other], mate1)
    second = remote("pool1b", r.part.at[parity], r.part_in.at[parity], mate1)
    first.start()
    second.start()
    first.wait()
    r.chip[parity] = added(r.part[parity], r.part_in[parity])
    pool = []
    for i in range(2):
        rows = pl.ds(i * 128, 128)
        pool.append(remote("pool2" + "ab"[i], r.chip.at[parity, rows], r.chip_in.at[rows], mate2))
        pool[i].start()
    second.wait()
    r.chip[other] = added(r.part[other], r.part_in[other])

    rows = jnp.concatenate([r.coarse_bound[...], r.list_in[...]], axis=1)
    both = jnp.concatenate([r.chip[0], r.chip[1]], axis=1)
    picked = half_of(rows >> 9, dot(both, onehot(rows & 511, 512)))
    r.rim_out[...] = picked.T.astype(BF).reshape(4, 64, 128)
    rims = (
        remote("rim0", r.rim_out.at[0], r.rim_in.at[1, 0], down),
        remote("rim1", r.rim_out.at[1], r.rim_in.at[0, 0], up),
        remote("rim2", r.rim_out.at[2], r.rim_in.at[1, 1], mate2_down),
        remote("rim3", r.rim_out.at[3], r.rim_in.at[0, 1], mate2_up),
    )

    @pl.when((q == 0) | (q == 3))
    def _():
        pl.semaphore_wait(here_sem, 1)

    @pl.when((q == 1) | (q == 2))
    def _():
        pl.semaphore_wait(here_sem, 2)

    for copy in rims:
        copy.start()

    table = jnp.concatenate([fine[:, :512], fine[:, 512:]], axis=0)
    picked = half_of(r.bound[...] >> 9, dot(table, r.bound_hot[...])).astype(BF)
    r.later_out[0] = picked[:, :256]
    r.later_out[1] = picked[:, 256:]
    later = (
        remote("later_l", r.later_out.at[0], r.later_in.at[1], left),
        remote("later_r", r.later_out.at[1], r.later_in.at[0], right),
    )
    for item in later:
        item.start()
    fine_tables(2, fine)
    later_own(range(4))

    w_send = r.w_edge[1, 1]
    tables = []
    for i in range(2):
        pool[i].wait()
        rows = slice(i * 128, i * 128 + 128)
        r.mine[i] = added(r.chip[parity, rows], r.chip_in[rows])
        r.coarse_table[parity, rows] = dot(w_send, r.mine[i]).astype(BF)
        block = r.coarse_table.at[parity, pl.ds(i * 128, 128)]
        tables.append(remote("table" + "ab"[i], block, block, mate1))
        tables[i].start()
    quarter = r.mine[half]
    recv_tables(1, quarter, 2)

    def coarse_part(b, side):
        send = index_row(r.coarse_send, b)
        inside = jnp.where(((send >> 8) & 1) == side, send & 255, -1)
        hot = onehot(jnp.where(send < 1024, inside, -1), 256)
        return half_of((send >> 9) & 1, dot(r.coarse_table[side], hot))

    w_edge = r.w_edge[1, 2]
    for b in range(2):
        joined = jnp.concatenate([r.recv_table[b], w_edge], axis=1)
        turned = r.coarse_edges[pl.ds(b * 1024, 1024), :].T
        columns = jnp.concatenate([onehot(index_row(r.coarse_recv, b), 128), turned], axis=0)
        r.before[:, block_lanes(b)] = dot(joined, columns) + coarse_part(b, parity)
    for item in tables:
        item.wait()
    for b in range(2):
        r.before[:, block_lanes(b)] += coarse_part(b, other)
    for copy in rims:
        copy.wait()
    rim = (r.rim_in[:, 0].astype(F32) + r.rim_in[:, 1].astype(F32)).astype(BF).reshape(128, 128)
    rim_table = dot_nt(w_send, rim).astype(BF)
    for b in range(2):
        send = index_row(r.coarse_send, b)
        outside = jnp.where(send >= 1024, send & 127, -1)
        r.before[:, block_lanes(b)] += dot(rim_table, onehot(outside, 128))

    messages(1, range(2), r.coarse_recv, r.coarse_live, False)
    r.fresh[1, parity, half] = node_update(1, range(2), quarter)
    own = r.fresh.at[1, parity, half]
    sender = 2 * parity + half
    across = remote("across", own, own, mate2)
    along = remote("along0", own, own, mate1)
    across.start()
    along.start()
    beside = (
        remote("ahead0", own, r.fresh.at[0, parity, half], ahead, COPIES.index("ahead0") + sender),
        remote("back0", own, r.fresh.at[2, parity, half], back, COPIES.index("back0") + sender),
    )
    later_own(range(4, 8))
    for item in beside:
        item.start()
    for item in later:
        item.wait()
    for i in range(2):
        r.halo_in[i * 128 : i * 128 + 128] = dot(r.w_edge[2, 1], r.later_in[i]).astype(BF)
    later_rim()
    across.wait()
    block = r.fresh.at[1, parity, 1 - half]
    forward = remote("along1", block, block, mate1)
    forward.start()
    raise_table(parity)
    found = dot(lifting(1, parity), r.cluster_hot[pl.ds(pl.multiple_of(parity * 256, 256), 256)])
    along.wait()
    forward.wait()
    raise_table(other)
    found += dot(lifting(1, other), r.cluster_hot[pl.ds(pl.multiple_of(other * 256, 256), 256)])
    r.state[...] = (r.state[...].astype(F32) + half_of(label >> 9, found)).astype(BF)

    recv_tables(2, r.state[...], 8)
    lifted_sums()
    for item in beside:
        item.wait_send()

    def arrive(name, group):
        for i in range(4):
            block = r.fresh.at[group, i // 2, i % 2]
            remote(name + str(i), block, block, left).wait_recv()

    @pl.when(q == 0)
    def _():
        arrive("ahead", 0)

    @pl.when(q == 3)
    def _():
        arrive("back", 2)

    @pl.when((q == 0) | (q == 3))
    def _():
        side = jnp.where(q == 0, 0, 1)
        raised = lift(2 * side, r.near_in[side][:1, :]).astype(BF)
        table = dot(r.w_edge[2, 1], raised).astype(BF)
        for b in range(8):
            send = index_row(r.fine_send, b)
            outside = jnp.where((send >> 8) == 4 + side, send & 255, -1)
            r.before[:, block_lanes(b)] += dot(table, onehot(outside, 256))

    messages(2, range(8), r.fine_recv, r.fine_live, False)
    out_ref[...] = node_update(2, range(8), r.state[...]).T


def local(
    nodes,
    fine_edges,
    fine_recv,
    fine_send,
    fine_live,
    bound_rows,
    cluster,
    coarse_edges,
    coarse_recv,
    coarse_send,
    coarse_live,
    coarse_bound,
    edge_in,
    edge_out,
    node_in,
    node_out,
):
    args = dict(
        nodes=nodes,
        edge_in=edge_in,
        bound=bound_rows,
        cluster=cluster.reshape(8, 128),
        fine_send=fine_send,
        fine_recv=fine_recv,
        fine_edges=fine_edges,
        coarse_bound=coarse_bound,
        edge_out=edge_out,
        fine_live=fine_live,
        node_in=node_in,
        node_out=node_out,
        coarse_edges=coarse_edges,
        coarse_recv=coarse_recv,
        coarse_send=coarse_send,
        coarse_live=coarse_live,
    )
    held = [(args[name].shape, args[name].dtype) for name in INPUTS] + list(SCRATCH.values())
    return pl.pallas_call(
        functools.partial(kernel, lax.axis_size("dom")),
        out_shape=jax.ShapeDtypeStruct((1024, 128), BF),
        in_specs=[pl.BlockSpec(memory_space=pl.ANY)] * len(INPUTS),
        out_specs=pl.BlockSpec(memory_space=pltpu.VMEM),
        scratch_shapes=[pltpu.VMEM(shape, dtype) for shape, dtype in held]
        + [
            pltpu.SemaphoreType.DMA((len(INPUTS) + 1,)),
            pltpu.SemaphoreType.DMA((8,)),
            pltpu.SemaphoreType.DMA((len(COPIES),)),
            pltpu.SemaphoreType.DMA((len(COPIES),)),
            pltpu.SemaphoreType.REGULAR,
        ],
        compiler_params=pltpu.CompilerParams(
            collective_id=0, has_side_effects=True, vmem_limit_bytes=56 << 20
        ),
    )(*[args[name] for name in INPUTS])


def solution(mesh):
    row = P("dom", None)
    return jax.shard_map(
        local,
        mesh=mesh,
        in_specs=(row,) * 6 + (P("dom"),) + (row,) * 5 + (P(),) * 4,
        out_specs=row,
        check_vma=False,
    )
```

```python
import functools

import jax
import jax.numpy as jnp
from jax import lax
from jax.experimental import pallas as pl
from jax.experimental.pallas import tpu as pltpu
from jax.sharding import PartitionSpec as P

MESH = pl.DeviceIdType.MESH
BF = jnp.bfloat16
F32 = jnp.float32
I32 = jnp.int32


def dot(a, b):
    return jnp.dot(a, b, preferred_element_type=F32)


def dot_nt(a, b):
    return lax.dot_general(a, b, (((1,), (1,)), ((), ())), preferred_element_type=F32)


def onehot(index, rows):
    numbers = lax.broadcasted_iota(jnp.int16, (rows, index.shape[1]), 0)
    return jnp.where(numbers == index.astype(jnp.int16), jnp.ones((), BF), jnp.zeros((), BF))


def half_of(upper, folded):
    return jnp.where(upper == 1, folded[128:], folded[:128])


def centred(weight_t):
    wide = weight_t.astype(F32)
    return (wide - jnp.mean(wide, axis=0, keepdims=True)).astype(BF)


def normalised(values):
    spread = jnp.mean(values * values, axis=0, keepdims=True)
    return values * lax.rsqrt(spread + 1e-05)


def index_row(ref, block):
    rows = ref[block * 8 : block * 8 + 8, :]
    return jnp.concatenate([rows[i : i + 1, :] for i in range(8)], axis=1)


def added(a, b):
    return (a.astype(F32) + b.astype(F32)).astype(BF)


def block_lanes(block):
    return slice(block * 1024, block * 1024 + 1024)


INPUTS = (
    "nodes",
    "edge_in",
    "bound",
    "cluster",
    "fine_send",
    "fine_recv",
    "fine_edges",
    "coarse_bound",
    "edge_out",
    "fine_live",
    "node_in",
    "node_out",
    "coarse_edges",
    "coarse_recv",
    "coarse_send",
    "coarse_live",
)
SCRATCH = dict(
    state=((128, 1024), BF),
    edges_t=((128, 8192), BF),
    before=((128, 8192), F32),
    aggregate=((8, 128, 128), F32),
    recv_table=((8, 128, 128), BF),
    own_table=((256, 512), BF),
    bound_hot=((512, 512), BF),
    cluster_hot=((512, 1024), BF),
    halo_out=((2, 128, 256), BF),
    halo_in=((256, 256), BF),
    later_out=((2, 128, 256), BF),
    later_in=((2, 128, 256), BF),
    w_edge=((3, 3, 128, 128), BF),
    w_message=((3, 128, 128), BF),
    w_node=((3, 128, 256), BF),
    w_update=((3, 128, 128), BF),
    digits=((32, 512), BF),
    sender_cluster=((8, 1024), F32),
    later_sums=((128, 8192), F32),
    lift_table=((2, 256, 256), BF),
    near_out=((2, 8, 256), I32),
    near_in=((2, 8, 256), I32),
    list_in=((1, 128), I32),
    count_out=((16, 512), F32),
    count_in=((3, 16, 512), F32),
    part=((2, 256, 256), BF),
    part_in=((2, 256, 256), BF),
    chip=((2, 256, 256), BF),
    chip_in=((256, 256), BF),
    mine=((2, 128, 256), BF),
    coarse_table=((2, 256, 256), BF),
    rim_out=((4, 64, 128), BF),
    rim_in=((2, 2, 64, 128), BF),
    fresh=((3, 2, 2, 128, 256), BF),
)
COPIES = (
    ["halo_l", "halo_r", "near_l", "near_r", "later_l", "later_r", "list"]
    + ["count1", "count2", "count3", "pool1a", "pool1b", "pool2a", "pool2b", "tablea", "tableb"]
    + ["rim0", "rim1", "rim2", "rim3", "across0", "across1", "along0", "along1", "along2"]
    + ["ahead0", "ahead1", "ahead2", "ahead3", "back0", "back1", "back2", "back3"]
)


class Refs:
    pass


def kernel(total, *refs):
    hbm = dict(zip(INPUTS, refs))
    out_ref = refs[len(INPUTS)]
    r = Refs()
    for name, ref in zip(INPUTS + tuple(SCRATCH), refs[len(INPUTS) + 1 :]):
        setattr(r, name, ref)
    load_sem, edge_sem, send_sem, recv_sem, here_sem = refs[-5:]

    me = lax.axis_index("dom")
    q = lax.rem(me, 4)
    base = me - q
    parity = lax.rem(q, 2)
    half = q // 2
    left = lax.rem(me + total - 1, total)
    right = lax.rem(me + 1, total)
    down = lax.rem(me + total - 4, total)
    up = lax.rem(me + 4, total)
    mate1 = base + q + 1 - 2 * parity
    mate2 = base + q + 2 - 4 * half
    mate3 = base + 3 - q
    mate2_down = lax.rem(mate2 + total - 4, total)
    mate2_up = lax.rem(mate2 + 4, total)
    ahead = lax.rem(base + 4, total)
    back = lax.rem(base + total - 1, total)

    def remote(name, src, dst, device, arrives=None):
        slot = COPIES.index(name)
        return pltpu.make_async_remote_copy(
            src_ref=src,
            dst_ref=dst,
            send_sem=send_sem.at[slot],
            recv_sem=recv_sem.at[slot if arrives is None else arrives],
            device_id=(device,),
            device_id_type=MESH,
        )

    barrier = pltpu.get_barrier_semaphore()

    def greet(device):
        pl.semaphore_signal(barrier, inc=1, device_id=(device,), device_id_type=MESH)

    loads = {}
    for i, name in enumerate(INPUTS):
        if name not in ("fine_edges", "edge_in"):
            loads[name] = pltpu.make_async_copy(hbm[name], getattr(r, name), load_sem.at[i])

    def edge_load(b):
        rows = pl.ds(b * 1024, 1024)
        return pltpu.make_async_copy(
            hbm["fine_edges"].at[rows], r.fine_edges.at[rows], edge_sem.at[b]
        )

    first_weights = pltpu.make_async_copy(
        hbm["edge_in"].at[0], r.edge_in.at[0], load_sem.at[len(INPUTS)]
    )
    loads["edge_in"] = pltpu.make_async_copy(
        hbm["edge_in"].at[pl.ds(1, 2)], r.edge_in.at[pl.ds(1, 2)], load_sem.at[1]
    )
    loads["nodes"].start()
    first_weights.start()
    loads["bound"].start()
    loads["cluster"].start()
    for device in (left, right, mate1, mate2, mate3):
        greet(device)

    def first_sums():
        w_edge = r.w_edge[0, 2]
        for b in range(8):
            send = index_row(r.fine_send, b)
            inside = jnp.where(send < 1024, send & 511, -1)
            gathered = half_of((send >> 9) & 1, dot(r.own_table[...], onehot(inside, 512)))
            edge_load(b).wait()
            turned = r.fine_edges[pl.ds(b * 1024, 1024), :].T
            r.edges_t[:, block_lanes(b)] = turned
            joined = jnp.concatenate([r.recv_table[b], w_edge], axis=1)
            columns = jnp.concatenate([onehot(index_row(r.fine_recv, b), 128), turned], axis=0)
            r.before[:, block_lanes(b)] = gathered + dot(joined, columns)

    def digits_of(upper, found):
        low = jnp.where(upper == 1, found[16:17], found[0:1])
        high = jnp.where(upper == 1, found[24:25], found[8:9])
        return low + 256.0 * high

    def later_own(blocks):
        table = jnp.concatenate([r.own_table[...], r.digits[...]], axis=0)
        for b in blocks:
            send = index_row(r.fine_send, b)
            upper = (send >> 9) & 1
            found = dot(table, onehot(jnp.where(send < 1024, send & 511, -1), 512))
            r.sender_cluster[b : b + 1, :] = digits_of(upper, found[256:])
            r.later_sums[:, block_lanes(b)] = half_of(upper, found[:256]) + dot(
                r.w_edge[2, 2], r.edges_t[:, block_lanes(b)]
            )

    def later_rim():
        near = r.near_in[...]
        digits = []
        for i in range(2):
            for digit in (near[i] & 255, near[i] >> 8):
                digits.append(digit.astype(F32).astype(BF))
        table = jnp.concatenate([r.halo_in[...]] + digits, axis=0)
        for b in range(8):
            send = index_row(r.fine_send, b)
            upper = (send >> 8) & 1
            found = dot(table, onehot(jnp.where(send >= 1024, send & 255, -1), 256))
            r.sender_cluster[b : b + 1, :] += digits_of(upper, found[256:])
            r.later_sums[:, block_lanes(b)] += half_of(upper, found[:256])

    def lifted_sums():
        table = jnp.concatenate([r.lift_table[0], r.lift_table[1]], axis=1)
        for b in range(8):
            place = index_row(r.fine_send, b) >> 8
            cluster = r.sender_cluster[b : b + 1, :].astype(I32)
            beside = ((place == 4) & (q == 0)) | ((place == 5) & (q == 3))
            found = dot(table, onehot(jnp.where(beside, -1, cluster & 511), 512))
            r.before[:, block_lanes(b)] = (
                r.later_sums[:, block_lanes(b)]
                + half_of(cluster >> 9, found)
                + dot(r.recv_table[b], onehot(index_row(r.fine_recv, b), 128))
            )

    def fine_rim():
        for b in range(8):
            send = index_row(r.fine_send, b)
            outside = jnp.where(send >= 1024, send & 255, -1)
            r.before[:, block_lanes(b)] += half_of(
                (send >> 8) & 1, dot(r.halo_in[...], onehot(outside, 256))
            )

    def messages(layer, blocks, recv_ref, live_ref, keep):
        w_message = r.w_message[layer]
        for b in blocks:
            lanes = block_lanes(b)
            active = jnp.maximum(r.before[:, lanes], 0.0).astype(BF)
            message = normalised(dot(w_message, active)).astype(BF)
            if keep:
                r.edges_t[:, lanes] = (
                    r.edges_t[:, lanes].astype(F32) + message.astype(F32)
                ).astype(BF)
            target = jnp.where(index_row(live_ref, b) == 1, index_row(recv_ref, b), -1)
            r.aggregate[b] = dot_nt(message, onehot(target, 128))

    def node_update(layer, blocks, own):
        totals = jnp.concatenate([r.aggregate[b] for b in blocks], axis=1)
        joined = jnp.concatenate([own, totals.astype(BF)], axis=0)
        hidden = jnp.maximum(dot(r.w_node[layer], joined), 0.0).astype(BF)
        change = normalised(dot(r.w_update[layer], hidden))
        return (own.astype(F32) + change).astype(BF)

    def fine_tables(layer, own):
        table = dot(r.w_edge[layer, 1], own).astype(BF)
        r.own_table[:128, :] = table[:, :512]
        r.own_table[128:, :] = table[:, 512:]

    def recv_tables(layer, own, blocks):
        table = dot(r.w_edge[layer, 0], own).astype(BF)
        for b in range(blocks):
            r.recv_table[b] = table[:, b * 128 : (b + 1) * 128]

    def lifting(group, side):
        return r.fresh[group, side].reshape(256, 256)

    def raise_table(side):
        for i in range(2):
            rows = slice(i * 128, i * 128 + 128)
            r.lift_table[side, rows] = dot(r.w_edge[2, 1], r.fresh[1, side, i]).astype(BF)

    def lift(group, index):
        hot = onehot(index & 511, 512)
        found = dot(lifting(group, 0), hot[:256]) + dot(lifting(group, 1), hot[256:])
        return half_of(index >> 9, found)

    loads["nodes"].wait()
    first_weights.wait()
    loads["bound"].wait()
    for name in INPUTS[4:] + ("edge_in",):
        if name == "fine_edges":
            for b in range(8):
                edge_load(b).start()
        else:
            loads[name].start()
    r.state[...] = r.nodes[...].T
    r.w_edge[0, 1] = r.edge_in[0, 1].T
    fine_tables(0, r.state[...])
    rows = r.bound[...]
    r.bound_hot[...] = onehot(rows & 511, 512)
    picked = half_of(rows >> 9, dot(r.own_table[...], r.bound_hot[...])).astype(BF)
    r.halo_out[0] = picked[:, :256]
    r.halo_out[1] = picked[:, 256:]
    halo = (
        remote("halo_l", r.halo_out.at[0], r.halo_in.at[pl.ds(128, 128)], left),
        remote("halo_r", r.halo_out.at[1], r.halo_in.at[pl.ds(0, 128)], right),
    )

    pl.semaphore_wait(barrier, 5)
    for copy in halo:
        copy.start()
    r.w_edge[0, 0] = r.edge_in[0, 0].T
    r.w_edge[0, 2] = r.edge_in[0, 2].T

    loads["cluster"].wait()
    label = index_row(r.cluster, 0)
    digits = []
    for columns in (label[:, :512], label[:, 512:]):
        for digit in (columns & 255, columns >> 8):
            digits.append(jnp.broadcast_to(digit.astype(F32), (8, 512)).astype(BF))
    r.digits[...] = jnp.concatenate(digits, axis=0)
    found = dot(r.digits[...], r.bound_hot[...])
    upper = jnp.broadcast_to(rows >> 9, (8, 512)) == 1
    low = jnp.where(upper, found[16:24], found[0:8])
    high = jnp.where(upper, found[24:32], found[8:16])
    near = (low + 256.0 * high).astype(I32)
    r.near_out[0] = near[:, :256]
    r.near_out[1] = near[:, 256:]
    r.cluster_hot[...] = onehot(label & 511, 512)
    members = lax.broadcasted_iota(I32, (16, 1024), 0) // 8 == (label >> 9)
    r.count_out[...] = dot_nt(jnp.where(members, 1.0, 0.0).astype(BF), r.cluster_hot[...])
    recv_tables(0, r.state[...], 8)
    loads["coarse_bound"].wait()
    early = (
        remote("near_l", r.near_out.at[0], r.near_in.at[1], left),
        remote("near_r", r.near_out.at[1], r.near_in.at[0], right),
        remote("count1", r.count_out, r.count_in.at[0], mate1),
        remote("count2", r.count_out, r.count_in.at[1], mate2),
        remote("count3", r.count_out, r.count_in.at[2], mate3),
        remote("list", r.coarse_bound, r.list_in, mate2),
    )
    for copy in early:
        copy.start()

    loads["fine_send"].wait()
    loads["fine_recv"].wait()

    first_sums()
    for name in INPUTS[8:] + ("edge_in",):
        loads[name].wait()
    for layer in range(3):
        if layer:
            for i in range(3):
                r.w_edge[layer, i] = r.edge_in[layer, i].T
        r.w_message[layer] = centred(r.edge_out[layer].T)
        r.w_node[layer] = r.node_in[layer].T
        r.w_update[layer] = centred(r.node_out[layer].T)
    for copy in halo:
        copy.wait()

    @pl.when((q == 0) | (q == 3))
    def _():
        for device in (mate1, mate2, mate3):
            pl.semaphore_signal(here_sem, inc=1, device_id=(device,), device_id_type=MESH)

    fine_rim()
    messages(0, range(8), r.fine_recv, r.fine_live, True)
    r.state[...] = node_update(0, range(8), r.state[...])

    for copy in early:
        copy.wait()
    share = 1.0 / jnp.maximum(r.count_out[...] + r.count_in[0] + r.count_in[1] + r.count_in[2], 1.0)
    fine = r.state[...]
    nothing = jnp.zeros_like(fine)
    folded = jnp.concatenate(
        [jnp.where(label < 512, fine, nothing), jnp.where(label < 512, nothing, fine)], axis=0
    )
    sums = dot_nt(folded, r.cluster_hot[...])
    for i in range(2):
        means = (sums[i * 128 : i * 128 + 128] * share[i * 8 : i * 8 + 1]).astype(BF)
        for j in range(2):
            r.part[j, i * 128 : i * 128 + 128] = means[:, j * 256 : j * 256 + 256]
    other = 1 - parity
    first = remote("pool1a", r.part.at[other], r.part_in.at[other], mate1)
    second = remote("pool1b", r.part.at[parity], r.part_in.at[parity], mate1)
    first.start()
    second.start()
    first.wait()
    r.chip[parity] = added(r.part[parity], r.part_in[parity])
    pool = []
    for i in range(2):
        rows = pl.ds(i * 128, 128)
        pool.append(remote("pool2" + "ab"[i], r.chip.at[parity, rows], r.chip_in.at[rows], mate2))
        pool[i].start()
    second.wait()
    r.chip[other] = added(r.part[other], r.part_in[other])

    rows = jnp.concatenate([r.coarse_bound[...], r.list_in[...]], axis=1)
    both = jnp.concatenate([r.chip[0], r.chip[1]], axis=1)
    picked = half_of(rows >> 9, dot(both, onehot(rows & 511, 512)))
    r.rim_out[...] = picked.T.astype(BF).reshape(4, 64, 128)
    rims = (
        remote("rim0", r.rim_out.at[0], r.rim_in.at[1, 0], down),
        remote("rim1", r.rim_out.at[1], r.rim_in.at[0, 0], up),
        remote("rim2", r.rim_out.at[2], r.rim_in.at[1, 1], mate2_down),
        remote("rim3", r.rim_out.at[3], r.rim_in.at[0, 1], mate2_up),
    )

    @pl.when((q == 0) | (q == 3))
    def _():
        pl.semaphore_wait(here_sem, 1)

    @pl.when((q == 1) | (q == 2))
    def _():
        pl.semaphore_wait(here_sem, 2)

    for copy in rims:
        copy.start()

    table = jnp.concatenate([fine[:, :512], fine[:, 512:]], axis=0)
    picked = half_of(r.bound[...] >> 9, dot(table, r.bound_hot[...])).astype(BF)
    r.later_out[0] = picked[:, :256]
    r.later_out[1] = picked[:, 256:]
    later = (
        remote("later_l", r.later_out.at[0], r.later_in.at[1], left),
        remote("later_r", r.later_out.at[1], r.later_in.at[0], right),
    )
    for item in later:
        item.start()
    fine_tables(2, fine)
    later_own(range(4))

    w_send = r.w_edge[1, 1]
    tables = []
    for i in range(2):
        pool[i].wait()
        rows = slice(i * 128, i * 128 + 128)
        r.mine[i] = added(r.chip[parity, rows], r.chip_in[rows])
        r.coarse_table[parity, rows] = dot(w_send, r.mine[i]).astype(BF)
        block = r.coarse_table.at[parity, pl.ds(i * 128, 128)]
        tables.append(remote("table" + "ab"[i], block, block, mate1))
        tables[i].start()
    quarter = r.mine[half]
    recv_tables(1, quarter, 2)

    def coarse_part(b, side):
        send = index_row(r.coarse_send, b)
        inside = jnp.where(((send >> 8) & 1) == side, send & 255, -1)
        hot = onehot(jnp.where(send < 1024, inside, -1), 256)
        return half_of((send >> 9) & 1, dot(r.coarse_table[side], hot))

    w_edge = r.w_edge[1, 2]
    for b in range(2):
        joined = jnp.concatenate([r.recv_table[b], w_edge], axis=1)
        turned = r.coarse_edges[pl.ds(b * 1024, 1024), :].T
        columns = jnp.concatenate([onehot(index_row(r.coarse_recv, b), 128), turned], axis=0)
        r.before[:, block_lanes(b)] = dot(joined, columns) + coarse_part(b, parity)
    for item in tables:
        item.wait()
    for b in range(2):
        r.before[:, block_lanes(b)] += coarse_part(b, other)
    for copy in rims:
        copy.wait()
    rim = (r.rim_in[:, 0].astype(F32) + r.rim_in[:, 1].astype(F32)).astype(BF).reshape(128, 128)
    rim_table = dot_nt(w_send, rim).astype(BF)
    for b in range(2):
        send = index_row(r.coarse_send, b)
        outside = jnp.where(send >= 1024, send & 127, -1)
        r.before[:, block_lanes(b)] += dot(rim_table, onehot(outside, 128))

    messages(1, range(2), r.coarse_recv, r.coarse_live, False)
    r.fresh[1, parity, half] = node_update(1, range(2), quarter)
    own = r.fresh.at[1, parity, half]
    sender = 2 * parity + half
    pieces = [pl.ds(i * 64, 64) for i in range(2)]
    across = []
    for i, rows in enumerate(pieces):
        piece = r.fresh.at[1, parity, half, rows]
        across.append(remote("across" + str(i), piece, piece, mate2))
        across[i].start()
    along = remote("along0", own, own, mate1)
    along.start()
    beside = (
        remote("ahead0", own, r.fresh.at[0, parity, half], ahead, COPIES.index("ahead0") + sender),
        remote("back0", own, r.fresh.at[2, parity, half], back, COPIES.index("back0") + sender),
    )
    later_own(range(4, 8))
    for item in beside:
        item.start()
    for item in later:
        item.wait()
    for i in range(2):
        r.halo_in[i * 128 : i * 128 + 128] = dot(r.w_edge[2, 1], r.later_in[i]).astype(BF)
    later_rim()
    forward = []
    for i, rows in enumerate(pieces):
        across[i].wait()
        piece = r.fresh.at[1, parity, 1 - half, rows]
        forward.append(remote("along" + str(i + 1), piece, piece, mate1))
        forward[i].start()
    raise_table(parity)
    found = dot(lifting(1, parity), r.cluster_hot[pl.ds(pl.multiple_of(parity * 256, 256), 256)])
    along.wait()
    for item in forward:
        item.wait()
    raise_table(other)
    found += dot(lifting(1, other), r.cluster_hot[pl.ds(pl.multiple_of(other * 256, 256), 256)])
    r.state[...] = (r.state[...].astype(F32) + half_of(label >> 9, found)).astype(BF)

    recv_tables(2, r.state[...], 8)
    lifted_sums()
    for item in beside:
        item.wait_send()

    def arrive(name, group):
        for i in range(4):
            block = r.fresh.at[group, i // 2, i % 2]
            remote(name + str(i), block, block, left).wait_recv()

    @pl.when(q == 0)
    def _():
        arrive("ahead", 0)

    @pl.when(q == 3)
    def _():
        arrive("back", 2)

    @pl.when((q == 0) | (q == 3))
    def _():
        side = jnp.where(q == 0, 0, 1)
        raised = lift(2 * side, r.near_in[side][:1, :]).astype(BF)
        table = dot(r.w_edge[2, 1], raised).astype(BF)
        for b in range(8):
            send = index_row(r.fine_send, b)
            outside = jnp.where((send >> 8) == 4 + side, send & 255, -1)
            r.before[:, block_lanes(b)] += dot(table, onehot(outside, 256))

    messages(2, range(8), r.fine_recv, r.fine_live, False)
    out_ref[...] = node_update(2, range(8), r.state[...]).T


def local(
    nodes,
    fine_edges,
    fine_recv,
    fine_send,
    fine_live,
    bound_rows,
    cluster,
    coarse_edges,
    coarse_recv,
    coarse_send,
    coarse_live,
    coarse_bound,
    edge_in,
    edge_out,
    node_in,
    node_out,
):
    args = dict(
        nodes=nodes,
        edge_in=edge_in,
        bound=bound_rows,
        cluster=cluster.reshape(8, 128),
        fine_send=fine_send,
        fine_recv=fine_recv,
        fine_edges=fine_edges,
        coarse_bound=coarse_bound,
        edge_out=edge_out,
        fine_live=fine_live,
        node_in=node_in,
        node_out=node_out,
        coarse_edges=coarse_edges,
        coarse_recv=coarse_recv,
        coarse_send=coarse_send,
        coarse_live=coarse_live,
    )
    held = [(args[name].shape, args[name].dtype) for name in INPUTS] + list(SCRATCH.values())
    return pl.pallas_call(
        functools.partial(kernel, lax.axis_size("dom")),
        out_shape=jax.ShapeDtypeStruct((1024, 128), BF),
        in_specs=[pl.BlockSpec(memory_space=pl.ANY)] * len(INPUTS),
        out_specs=pl.BlockSpec(memory_space=pltpu.VMEM),
        scratch_shapes=[pltpu.VMEM(shape, dtype) for shape, dtype in held]
        + [
            pltpu.SemaphoreType.DMA((len(INPUTS) + 1,)),
            pltpu.SemaphoreType.DMA((8,)),
            pltpu.SemaphoreType.DMA((len(COPIES),)),
            pltpu.SemaphoreType.DMA((len(COPIES),)),
            pltpu.SemaphoreType.REGULAR,
        ],
        compiler_params=pltpu.CompilerParams(
            collective_id=0, has_side_effects=True, vmem_limit_bytes=56 << 20
        ),
    )(*[args[name] for name in INPUTS])


def solution(mesh):
    row = P("dom", None)
    return jax.shard_map(
        local,
        mesh=mesh,
        in_specs=(row,) * 6 + (P("dom"),) + (row,) * 5 + (P(),) * 4,
        out_specs=row,
        check_vma=False,
    )
```
